512 devices in a mesh: clip: 32 (over x, y), seq: 16 (over z, core).
Axes of the slice: x: 4, y: 8, z: 8, core: 2. Of those that a mesh axis runs over, the one named last changes fastest.
Arguments:
- queries: bfloat16 [32, 2048, 4096], P('clip', 'seq'), may hold values from -34 to 34
- keys: bfloat16 [32, 2048, 4096], P('clip', 'seq'), may hold values from -6 to 6
- values: bfloat16 [32, 2048, 4096], P('clip', 'seq'), may hold values from -6 to 6
- frame_counts: int32 [128], P('clip'), may hold values from 1 to 4
- assignment: int32 [32], P('clip'), may hold values from 0 to 127
- timesteps: int32 [32], P('clip'), may hold values from 0 to 999
- gate_gain: float32 [4096], replicated, may hold values from -3 to 3
Outputs:
- attended: bfloat16 [32, 2048, 4096], P('clip', 'seq')
The draws below stay inside these ranges and needn't reach their ends.
All inputs are finite; a program needn't handle non-finite values.
Results may differ from the reference program's by a relative error of at most 0.0086.
Values may be sent and summed in bfloat16 or wider, within the bound.
A program may use at most 128 MiB of HBM per device.

```python
import jax
import jax.numpy as jnp
from jax import lax

HEADS = 32
HD = 128
FRAME_TOK = 448
GRID_W = 28
CLIPS = 32
TOKENS = 2048


def query_key_draw(key):
    query_key = jax.random.fold_in(key, 11)
    key_key = jax.random.fold_in(key, 12)
    shape = (CLIPS, TOKENS, HEADS * HD)
    keys = jnp.clip(jax.random.normal(key_key, shape, jnp.float32), -6.0, 6.0)
    queries = jnp.clip(2.5 * jax.random.normal(query_key, shape, jnp.float32), -15.0, 15.0)
    return (queries, keys)


def draw_queries(key, part):
    return query_key_draw(key)[0].astype(jnp.bfloat16)


def draw_keys(key, part):
    return query_key_draw(key)[1].astype(jnp.bfloat16)


def set_ends(result, own_key, smallest, top_value):
    longest = result.shape.index(max(result.shape))
    spots = []
    for shift in (0, 1):
        where = [jax.random.randint(jax.random.fold_in(own_key, axis), (), 0, length) for axis, length in enumerate(result.shape)]
        where[longest] = (where[longest] + shift) % result.shape[longest]
        spots.append(tuple(where))
    return result.at[spots[0]].set(smallest).at[spots[1]].set(top_value)


def level_of(own_key, extent, cuts, least, high):
    factor_of, own = 1.0, jax.random.fold_in(own_key, 6)
    for axis_at, blocks in cuts:
        draws = jnp.exp(jax.random.uniform(jax.random.fold_in(own, axis_at), (blocks,), jnp.float32, least / len(cuts), high / len(cuts)))
        factor_of = factor_of * jnp.repeat(draws, extent[axis_at] // blocks).reshape([-1 if axis == axis_at else 1 for axis in range(len(extent))])
    return factor_of


def centred(key, extent, spread, reach, split=(), kind=jnp.bfloat16):
    loudness = level_of(key, extent, split, -0.22, 0.18) if split else 1.0
    result = jax.random.normal(key, extent, jnp.float32) * spread * loudness
    return jnp.minimum(jnp.maximum(result, -reach), reach).astype(kind)


def setup_inputs(seed: int = 0) -> dict:
    seeds = jax.random.split(jax.random.key(seed), 8)
    queries = draw_queries(jax.random.fold_in(seeds[7], 71), 0)
    keys = draw_keys(jax.random.fold_in(seeds[7], 71), 0)
    values = centred(seeds[2], (CLIPS, TOKENS, HEADS * HD), 1.0, 6.0, ((0, 32), (1, 16)))
    frame_counts = set_ends(jax.random.randint(seeds[3], (4 * CLIPS,), 1, TOKENS // FRAME_TOK + 1), jax.random.fold_in(seeds[3], 1), 1, (TOKENS // FRAME_TOK + 1) - 1).astype(jnp.int32)
    assignment = set_ends(jax.random.randint(seeds[4], (CLIPS,), 0, 4 * CLIPS), jax.random.fold_in(seeds[4], 1), 0, (4 * CLIPS) - 1).astype(jnp.int32)
    timesteps = set_ends(jax.random.randint(seeds[5], (CLIPS,), 0, 1000), jax.random.fold_in(seeds[5], 1), 0, 999).astype(jnp.int32)
    gate_gain = centred(seeds[6], (HEADS * HD,), 0.5, 3.0, (), jnp.float32)
    return {"queries": queries, "keys": keys, "values": values, "frame_counts": frame_counts, "assignment": assignment, "timesteps": timesteps, "gate_gain": gate_gain}


def rope_tables(count):
    position = jnp.arange(count, dtype=jnp.int32)
    frame = (position // FRAME_TOK).astype(jnp.float32)
    within = position % FRAME_TOK
    row_pos = (within // GRID_W).astype(jnp.float32)
    col_pos = (within % GRID_W).astype(jnp.float32)
    temporal = jnp.arange(22, dtype=jnp.float32)
    spatial = jnp.arange(21, dtype=jnp.float32)
    inv_time = 10000.0 ** (-2.0 * temporal / 44.0)
    inv_space = 10000.0 ** (-2.0 * spatial / 42.0)
    angles = jnp.concatenate([frame[:, None] * inv_time[None, :], row_pos[:, None] * inv_space[None, :], col_pos[:, None] * inv_space[None, :]], axis=1)
    return jnp.cos(angles), jnp.sin(angles)


def rotate(vectors, cosine, sine):
    half = vectors.shape[-1] // 2
    first = vectors[..., :half].astype(jnp.float32)
    second = vectors[..., half:].astype(jnp.float32)
    cos_b = cosine[:, None, :]
    sin_b = sine[:, None, :]
    return jnp.concatenate([first * cos_b - second * sin_b, first * sin_b + second * cos_b], axis=-1).astype(jnp.bfloat16)


def reference(queries, keys, values, frame_counts, assignment, timesteps, gate_gain):
    lengths = (frame_counts[assignment] * FRAME_TOK).astype(jnp.int32)
    fraction = timesteps.astype(jnp.float32) / 1000.0
    sigma = 5.0 * fraction / (1.0 + 4.0 * fraction)
    cosine, sine = rope_tables(TOKENS)
    scale = HD ** -0.5
    positions = jnp.arange(TOKENS, dtype=jnp.int32)

    def one_clip(items):
        query, key_in, value, length, level = items
        query = rotate(query.reshape(TOKENS, HEADS, HD), cosine, sine)
        key_in = rotate(key_in.reshape(TOKENS, HEADS, HD), cosine, sine)
        value = value.reshape(TOKENS, HEADS, HD)

        def one_head(head_items):
            q_head, k_head, v_head = head_items
            scores = jnp.dot(q_head, k_head.T, preferred_element_type=jnp.float32) * scale
            scores = jnp.where(positions[None, :] < length, scores, -jnp.inf)
            top = jnp.max(scores, axis=-1, keepdims=True)
            weights = jnp.exp(scores - top)
            total = jnp.sum(weights, axis=-1)
            mixed = jnp.dot(weights.astype(jnp.bfloat16), v_head, preferred_element_type=jnp.float32) / total[:, None]
            return mixed.astype(jnp.bfloat16)

        mixed = lax.map(one_head, (jnp.transpose(query, (1, 0, 2)), jnp.transpose(key_in, (1, 0, 2)), jnp.transpose(value, (1, 0, 2))))
        mixed = jnp.transpose(mixed, (1, 0, 2)).reshape(TOKENS, HEADS * HD).astype(jnp.float32)
        gated = mixed * (1.0 + level * gate_gain[None, :])
        return jnp.where(positions[:, None] < length, gated, 0.0).astype(jnp.bfloat16)

    return lax.map(one_clip, (queries, keys, values, lengths, sigma))
```

```python
import math

import jax
import jax.numpy as jnp
import numpy as np
from jax import lax
from jax.experimental import pallas as pl
from jax.experimental.pallas import tpu as pltpu
from jax.sharding import PartitionSpec as P

HD = 128
FRAME_TOK = 448
GRID_W = 28
LIVE = 1792
TOK = 128
EXTRA0 = 3584
MESH = pl.DeviceIdType.MESH
EXP_SCALE = HD ** (-0.5) * math.log2(math.e)
BF = jnp.bfloat16
F32 = jnp.float32
WIDE = 256


def rope_tables():
    position = np.arange(LIVE)
    frame = (position // FRAME_TOK).astype(np.float32)
    within = position % FRAME_TOK
    row_pos = (within // GRID_W).astype(np.float32)
    col_pos = (within % GRID_W).astype(np.float32)
    inv_time = 10000.0 ** (-2.0 * np.arange(22) / 44.0)
    inv_space = 10000.0 ** (-2.0 * np.arange(21) / 42.0)
    angles = np.concatenate(
        [
            frame[:, None] * inv_time[None, :],
            row_pos[:, None] * inv_space[None, :],
            col_pos[:, None] * inv_space[None, :],
        ],
        axis=1,
    )
    cosine, sine = np.cos(angles), np.sin(angles)
    table = np.stack(
        [np.concatenate([cosine, cosine], axis=1), np.concatenate([-sine, sine], axis=1)]
    )
    return table.astype(np.float32)


def kernel(
    nx,
    ny,
    compute,
    q,
    k,
    v,
    counts,
    assignment,
    timesteps,
    gain,
    table,
    out,
    qb,
    kb,
    vb,
    ob,
    qx,
    kx,
    vx,
    ox,
    kr,
    vt,
    sbuf,
    rel,
    relx,
    relo,
    relox,
    ybuf,
    xbuf,
    tab,
    lenb,
    zbuf,
    ss,
    sx,
    rs,
    rx,
    so,
    sox,
    ro,
    rox,
    rr,
    rrx,
    fs,
    fsx,
    rro,
    rrox,
    fso,
    fsox,
    ysend,
    yrecv,
    xsend,
    xrecv,
    loc,
):
    cl = lax.axis_index("clip")
    i = lax.axis_index("seq")
    z = i // 2
    c = i % 2
    y = cl % ny
    x = cl // ny
    has_x = (c == 0) & (z % 3 != 0) & (i < 14)
    slot = z - z // 4
    my_e = z - 1 - z // 3

    def chip_at(t):
        mag = (4 - t // 2) * ((t + 7) // 8)
        return (z + mag * (1 - 2 * (t % 2)) + 8) % 8

    def rcopy(src, dst, send, recv, j):
        return pltpu.make_async_remote_copy(
            src, dst, send, recv, device_id={"seq": j}, device_id_type=MESH
        )

    def arrived(view, sem):
        pltpu.make_async_copy(view, view, sem).wait()

    def rows_of(j, n=TOK):
        return pl.ds(pl.multiple_of(j * n, n), n)

    def cols(start, n):
        return pl.ds(pl.multiple_of(start, 128), n)

    barrier = pltpu.get_barrier_semaphore()

    def greet(axis, j):
        pl.semaphore_signal(barrier, inc=1, device_id={axis: j}, device_id_type=MESH)

    for dy in range(1, ny):
        greet("clip", x * ny + (y + dy) % ny)
    for dx in range(1, nx):
        greet("clip", ((x + dx) % nx) * ny + y)
    near = ny - 1 + nx - 1

    @pl.when(i < 14)
    def _():
        def one(t, carry):
            w = chip_at(t)
            for cc in (0, 1):

                @pl.when((w != 7) & (t != 1) & (2 * w + cc != i))
                def _():
                    greet("seq", 2 * w + cc)

                @pl.when((w != 7) & (t == 1))
                def _():
                    greet("seq", 14 + cc)

            return carry

        lax.fori_loop(0, 8, one, 0)
        pl.semaphore_wait(barrier, near + 13)

    @pl.when(i >= 14)
    def _():
        def one(n, carry):
            greet("seq", n + 2 * (n // 6))
            return carry

        lax.fori_loop(0, 12, one, 0)
        pl.semaphore_wait(barrier, near + 12)

    lane = lax.broadcasted_iota(jnp.int32, (8, 128), 1)
    mine = jnp.zeros((8, 128), jnp.int32)
    for m in range(4):
        mine = jnp.where(lane == 4 * cl + m, counts[m], mine)
    ybuf[y] = mine

    def ycopy(dy):
        return pltpu.make_async_remote_copy(
            ybuf.at[y],
            ybuf.at[y],
            ysend.at[dy],
            yrecv.at[y],
            device_id={"clip": x * ny + (y + dy) % ny},
            device_id_type=MESH,
        )

    def xcopy(dx):
        return pltpu.make_async_remote_copy(
            xbuf.at[x],
            xbuf.at[x],
            xsend.at[dx],
            xrecv.at[x],
            device_id={"clip": ((x + dx) % nx) * ny + y},
            device_id_type=MESH,
        )

    for dy in range(1, ny):
        ycopy(dy).start()

    arrays = ((k, kb, kx), (v, vb, vx), (q, qb, qx))

    def each_send(a, act):
        src, buf, bx = arrays[a]

        def one(tt, carry):
            t = (tt + 1) % 8
            w = chip_at(t)
            e = w - 1 - w // 3

            @pl.when((w != 7) & (t == 1))
            def _():
                act(
                    rcopy(
                        src.at[0, :, cols(512 * w, 512)],
                        rel.at[a, slot],
                        ss.at[a, 2 * w],
                        rr.at[a, slot],
                        14 + c,
                    )
                )

                @pl.when(w % 3 != 0)
                def _():
                    act(
                        rcopy(
                            src.at[0, :, cols(EXTRA0 + 128 * e, 128)],
                            relx.at[a, slot],
                            sx.at[a, e],
                            rrx.at[a, slot],
                            14 + c,
                        )
                    )

            @pl.when((w != 7) & (t != 1))
            def _():
                for cc in (0, 1):
                    j = 2 * w + cc

                    @pl.when(j != i)
                    def _():
                        act(
                            rcopy(
                                src.at[0, :, cols(256 * j, 256)],
                                buf.at[rows_of(i)],
                                ss.at[a, j],
                                rs.at[a, i],
                                j,
                            )
                        )

                @pl.when((w % 3 != 0) & (2 * w != i))
                def _():
                    act(
                        rcopy(
                            src.at[0, :, cols(EXTRA0 + 128 * e, 128)],
                            bx.at[rows_of(i)],
                            sx.at[a, e],
                            rx.at[a, i],
                            2 * w,
                        )
                    )

            return carry

        lax.fori_loop(0, 8, one, 0)

    def own_copy(a):
        src, buf, bx = arrays[a]
        pltpu.make_async_copy(
            src.at[0, :, cols(256 * i, 256)], buf.at[rows_of(i)], rs.at[a, i]
        ).start()

        @pl.when(has_x)
        def _():
            pltpu.make_async_copy(
                src.at[0, :, cols(EXTRA0 + 128 * my_e, 128)], bx.at[rows_of(i)], rx.at[a, i]
            ).start()

    def await_block(a, w):
        _, buf, bx = arrays[a]
        for cc in (0, 1):
            j = 2 * w + cc
            arrived(buf.at[rows_of(j)], rs.at[a, j])

            @pl.when(has_x)
            def _():
                arrived(bx.at[rows_of(j)], rx.at[a, j])

    def turn(block, w):
        part = pl.ds(pl.multiple_of(w * WIDE, WIDE), WIDE)
        return block * tab[0, part] + pltpu.roll(block, HD // 2, 1) * tab[1, part]

    def positions(shape, dim):
        return lax.broadcasted_iota(jnp.int32, shape, dim).astype(F32)

    def start(copy):
        copy.start()

    def each_result(w, t, act):
        part = pl.ds(pl.multiple_of(w * WIDE, WIDE), WIDE)

        @pl.when(t == 1)
        def _():
            act(rcopy(ob.at[part], relo.at[slot], so.at[2 * w], rro.at[slot], 14 + c))

            @pl.when(has_x)
            def _():
                act(rcopy(ox.at[part], relox.at[slot], sox.at[2 * w], rrox.at[slot], 14 + c))

        @pl.when(t != 1)
        def _():
            for cc in (0, 1):
                j = 2 * w + cc

                @pl.when(j != i)
                def _():
                    act(
                        rcopy(
                            ob.at[rows_of(j)],
                            out.at[0, :, cols(256 * i, 256)],
                            so.at[j],
                            ro.at[i],
                            j,
                        )
                    )

                    @pl.when(has_x)
                    def _():
                        act(
                            rcopy(
                                ox.at[rows_of(j)],
                                out.at[0, :, cols(EXTRA0 + 128 * my_e, 128)],
                                sox.at[j],
                                rox.at[my_e],
                                j,
                            )
                        )

    def gate_of(head):
        fraction = jnp.full((1, HD), timesteps[0], jnp.int32).astype(F32) / 1000.0
        sigma = 5.0 * fraction / (1.0 + 4.0 * fraction)
        return 1.0 + sigma * gain[pl.ds(head, 1), :]

    def attend(h, block, w, head):
        q_rot = turn(block.astype(F32), w).astype(BF)
        top = None
        for n in range(LIVE // WIDE):
            part = pl.ds(n * WIDE, WIDE)
            s = lax.dot_general(
                kr[h, part], q_rot, (((1,), (1,)), ((), ())), preferred_element_type=F32
            )
            sbuf[h, part] = s
            high = jnp.max(s.reshape(WIDE // 8, 8, WIDE), axis=0)
            top = high if top is None else jnp.maximum(top, high)
        top = jnp.max(top, axis=0, keepdims=True)
        total = None
        for n in range(LIVE // WIDE):
            part = pl.ds(n * WIDE, WIDE)
            p = jnp.exp2((sbuf[h, part] - top) * EXP_SCALE).astype(BF)
            term = jnp.dot(vt[h, :, part], p, preferred_element_type=F32)
            total = term if total is None else total + term
        mixed = total[:HD] * (1.0 / total[HD : HD + 1])
        mixed = jnp.transpose(mixed).astype(BF).astype(F32)
        pos = positions((WIDE, HD), 0) + (w * WIDE).astype(F32)
        return jnp.where(pos < lenb[0:1, 0:HD], mixed * gate_of(head), 0.0).astype(BF)

    @pl.when(i < 14)
    def _():
        table_copy = pltpu.make_async_copy(table, tab, loc.at[0])
        table_copy.start()
        for a in range(3):
            each_send(a, start)
            own_copy(a)
        table_copy.wait()

        def k_step(tt, carry):
            w = chip_at((8 - tt) % 8)

            @pl.when(w != 7)
            def _():
                part = pl.ds(pl.multiple_of(w * WIDE, WIDE), WIDE)
                await_block(0, w)
                for h in (0, 1):
                    kr[h, part] = turn(kb[part, h * HD : (h + 1) * HD].astype(F32), w).astype(BF)

                @pl.when(has_x)
                def _():
                    kr[2, part] = turn(kx[part].astype(F32), w).astype(BF)

            return carry

        lax.fori_loop(0, 8, k_step, 0)

    for dy in range(1, ny):
        o = (y + dy) % ny
        arrived(ybuf.at[o], yrecv.at[o])
    xbuf[x] = jnp.sum(ybuf[...], axis=0)
    for dx in range(1, nx):
        xcopy(dx).start()
    for dx in range(1, nx):
        o = (x + dx) % nx
        arrived(xbuf.at[o], xrecv.at[o])
    pool = jnp.sum(xbuf[...], axis=0)
    picked = jnp.where(lane == assignment[0], pool, 0).astype(F32)
    length = jnp.sum(picked, axis=1, keepdims=True) * float(FRAME_TOK)
    lenb[...] = jnp.broadcast_to(length, (8, WIDE))
    for dy in range(1, ny):
        ycopy(dy).wait_send()
    for dx in range(1, nx):
        xcopy(dx).wait_send()

    @pl.when(i < 14)
    def _():
        for n in range(1, 4):
            part = pl.ds(n * FRAME_TOK, FRAME_TOK)
            live = positions((FRAME_TOK, HD), 0) + float(n * FRAME_TOK) < lenb[0:1, 0:HD]
            for h in range(3):

                def patch(h=h):
                    first = kr[h, 0:16].astype(F32)[0:1]
                    kr[h, part] = jnp.where(live, kr[h, part].astype(F32), first).astype(BF)

                if h < 2:
                    patch()
                else:
                    pl.when(has_x)(patch)

        def v_step(tt, carry):
            w = chip_at((8 - tt) % 8)

            @pl.when(w != 7)
            def _():
                part = pl.ds(pl.multiple_of(w * WIDE, WIDE), WIDE)
                await_block(1, w)
                pos = positions((1, WIDE), 1) + (w * WIDE).astype(F32)
                live = pos < lenb[0:1]
                ones = jnp.broadcast_to(jnp.where(live, 1.0, 0.0), (16, WIDE)).astype(BF)

                def put(h, block):
                    turned = jnp.transpose(block.astype(F32))
                    vt[h, 0:HD, part] = jnp.where(live, turned, 0.0).astype(BF)
                    vt[h, HD : HD + 16, part] = ones

                for h in (0, 1):
                    put(h, vb[part, h * HD : (h + 1) * HD])

                @pl.when(has_x)
                def _():
                    put(2, vx[part])

            return carry

        lax.fori_loop(0, 8, v_step, 0)

        def q_step(t, carry):
            w = chip_at(t)

            @pl.when(w != 7)
            def _():
                part = pl.ds(pl.multiple_of(w * WIDE, WIDE), WIDE)
                await_block(2, w)
                if compute:
                    for h in (0, 1):
                        lanes = slice(h * HD, (h + 1) * HD)
                        ob[part, lanes] = attend(h, qb[part, lanes], w, 2 * i + h)

                    @pl.when(has_x)
                    def _():
                        ox[part] = attend(2, qx[part], w, 28 + my_e)

                each_result(w, t, start)

            return carry

        lax.fori_loop(0, 8, q_step, 0)

        own = [pltpu.make_async_copy(ob.at[rows_of(i)], out.at[0, :, cols(256 * i, 256)], loc.at[1])]
        own[0].start()
        own_x = pltpu.make_async_copy(
            ox.at[rows_of(i)], out.at[0, :, cols(EXTRA0 + 128 * my_e, 128)], loc.at[2]
        )

        @pl.when(has_x)
        def _():
            own_x.start()

        for a in range(3):
            each_send(a, lambda copy: copy.wait_send())

        def drain(t, carry):
            w = chip_at(t)

            @pl.when(w != 7)
            def _():
                each_result(w, t, lambda copy: copy.wait_send())

            return carry

        lax.fori_loop(0, 8, drain, 0)
        own[0].wait()

        @pl.when(has_x)
        def _():
            own_x.wait()

        def gather(j, carry):
            @pl.when(j != i)
            def _():
                arrived(out.at[0, :, cols(256 * j, 256)], ro.at[j])

            return carry

        lax.fori_loop(0, 14, gather, 0)

        def gather_x(e, carry):
            @pl.when(jnp.logical_not(has_x & (e == my_e)))
            def _():
                arrived(out.at[0, :, cols(EXTRA0 + 128 * e, 128)], rox.at[e])

            return carry

        lax.fori_loop(0, 4, gather_x, 0)

    @pl.when(i >= 14)
    def _():
        zbuf[...] = jnp.zeros_like(zbuf)
        blank = [
            pltpu.make_async_copy(zbuf, out.at[0, n * 16 : (n + 1) * 16], loc.at[n])
            for n in range(8)
        ]
        for copy in blank:
            copy.start()

        def forward(a, n, act):
            _, buf, bx = arrays[a]
            o = n + (n + 1) // 4
            w = (o + 4) % 8
            j = 2 * o + c
            for cc in (0, 1):
                act(
                    rcopy(
                        rel.at[a, n, :, cc * 256 : (cc + 1) * 256],
                        buf.at[rows_of(j)],
                        fs.at[a, n, cc],
                        rs.at[a, j],
                        2 * w + cc,
                    )
                )

            @pl.when(w % 3 != 0)
            def _():
                act(rcopy(relx.at[a, n], bx.at[rows_of(j)], fsx.at[a, n], rx.at[a, j], 2 * w))

        for a in range(3):

            def pass_on(n, carry, a=a):
                o = n + (n + 1) // 4
                w = (o + 4) % 8
                arrived(rel.at[a, n], rr.at[a, n])

                @pl.when(w % 3 != 0)
                def _():
                    arrived(relx.at[a, n], rrx.at[a, n])

                forward(a, n, start)
                return carry

            lax.fori_loop(0, 6, pass_on, 0)

        def forward_result(n, act):
            o = n + (n + 1) // 4
            w = (o + 4) % 8
            j = 2 * o + c
            e = o - 1 - o // 3
            for cc in (0, 1):
                act(
                    rcopy(
                        relo.at[n, cc * TOK : (cc + 1) * TOK],
                        out.at[0, :, cols(256 * j, 256)],
                        fso.at[n, cc],
                        ro.at[j],
                        2 * w + cc,
                    )
                )

            @pl.when((o % 3 != 0) & (c == 0))
            def _():
                for cc in (0, 1):
                    act(
                        rcopy(
                            relox.at[n, cc * TOK : (cc + 1) * TOK],
                            out.at[0, :, cols(EXTRA0 + 128 * e, 128)],
                            fsox.at[n, cc],
                            rox.at[e],
                            2 * w + cc,
                        )
                    )

        def pass_result(n, carry):
            o = n + (n + 1) // 4
            arrived(relo.at[n], rro.at[n])

            @pl.when((o % 3 != 0) & (c == 0))
            def _():
                arrived(relox.at[n], rrox.at[n])

            forward_result(n, start)
            return carry

        lax.fori_loop(0, 6, pass_result, 0)

        def finish(n, carry):
            for a in range(3):
                forward(a, n, lambda copy: copy.wait_send())
            forward_result(n, lambda copy: copy.wait_send())
            return carry

        lax.fori_loop(0, 6, finish, 0)
        for copy in blank:
            copy.wait()


def build(mesh, compute=True):
    clips = mesh.shape["clip"]
    ny = min(8, clips)
    nx = clips // ny
    dma = pltpu.SemaphoreType.DMA

    def local(queries, keys, values, frame_counts, assignment, timesteps, gate_gain):
        def call(*args):
            kernel(nx, ny, compute, *args)

        anywhere = pl.BlockSpec(memory_space=pl.ANY)
        scalars = pl.BlockSpec(memory_space=pltpu.SMEM)
        return pl.pallas_call(
            call,
            out_shape=jax.ShapeDtypeStruct(queries.shape, BF),
            in_specs=[anywhere] * 3
            + [scalars] * 3
            + [pl.BlockSpec(memory_space=pltpu.VMEM), anywhere],
            out_specs=anywhere,
            scratch_shapes=[pltpu.VMEM((LIVE, 256), BF)] * 4
            + [pltpu.VMEM((LIVE, HD), BF)] * 4
            + [
                pltpu.VMEM((3, LIVE, HD), BF),
                pltpu.VMEM((3, HD + 16, LIVE), BF),
                pltpu.VMEM((3, LIVE, WIDE), F32),
                pltpu.VMEM((3, 6, TOK, 512), BF),
                pltpu.VMEM((3, 6, TOK, HD), BF),
                pltpu.VMEM((6, WIDE, 256), BF),
                pltpu.VMEM((6, WIDE, HD), BF),
                pltpu.VMEM((ny, 8, 128), jnp.int32),
                pltpu.VMEM((nx, 8, 128), jnp.int32),
                pltpu.VMEM((2, LIVE, HD), F32),
                pltpu.VMEM((8, WIDE), F32),
                pltpu.VMEM((16, 4096), BF),
                dma((3, 14)),
                dma((3, 4)),
                dma((3, 14)),
                dma((3, 14)),
                dma((14,)),
                dma((14,)),
                dma((14,)),
                dma((4,)),
                dma((3, 6)),
                dma((3, 6)),
                dma((3, 6, 2)),
                dma((3, 6)),
                dma((6,)),
                dma((6,)),
                dma((6, 2)),
                dma((6, 2)),
                dma((8,)),
                dma((8,)),
                dma((4,)),
                dma((4,)),
                dma((8,)),
            ],
            compiler_params=pltpu.CompilerParams(
                collective_id=0, has_side_effects=True, vmem_limit_bytes=63 * 2**20
            ),
            cost_estimate=pl.CostEstimate(
                flops=4 * 1792 * 1792 * 256,
                bytes_accessed=8 * 2**20,
                transcendentals=2 * 1792 * 1792,
            ),
        )(
            queries,
            keys,
            values,
            frame_counts,
            assignment,
            timesteps,
            gate_gain.reshape(32, HD),
            jnp.asarray(rope_tables()),
        )

    tokens = P("clip", "seq", None)
    return jax.shard_map(
        local,
        mesh=mesh,
        in_specs=(tokens, tokens, tokens, P("clip"), P("clip"), P("clip"), P()),
        out_specs=tokens,
        check_vma=False,
    )


def solution(mesh):
    return build(mesh)
```

```python
import math

import jax
import jax.numpy as jnp
import numpy as np
from jax import lax
from jax.experimental import pallas as pl
from jax.experimental.pallas import tpu as pltpu
from jax.sharding import PartitionSpec as P

HD = 128
FRAME_TOK = 448
GRID_W = 28
LIVE = 1792
TOK = 128
EXTRA0 = 3584
MESH = pl.DeviceIdType.MESH
EXP_SCALE = HD ** (-0.5) * math.log2(math.e)
BF = jnp.bfloat16
F32 = jnp.float32
WIDE = 256


def rope_tables():
    position = np.arange(LIVE)
    frame = (position // FRAME_TOK).astype(np.float32)
    within = position % FRAME_TOK
    row_pos = (within // GRID_W).astype(np.float32)
    col_pos = (within % GRID_W).astype(np.float32)
    inv_time = 10000.0 ** (-2.0 * np.arange(22) / 44.0)
    inv_space = 10000.0 ** (-2.0 * np.arange(21) / 42.0)
    angles = np.concatenate(
        [
            frame[:, None] * inv_time[None, :],
            row_pos[:, None] * inv_space[None, :],
            col_pos[:, None] * inv_space[None, :],
        ],
        axis=1,
    )
    cosine, sine = np.cos(angles), np.sin(angles)
    table = np.stack(
        [np.concatenate([cosine, cosine], axis=1), np.concatenate([-sine, sine], axis=1)]
    )
    return table.astype(np.float32)


def kernel(
    nx,
    ny,
    q,
    k,
    v,
    counts,
    assignment,
    timesteps,
    gain,
    table,
    out,
    qb,
    kb,
    vb,
    ob,
    qx,
    kx,
    vx,
    ox,
    kr,
    vt,
    sbuf,
    rel,
    relx,
    relo,
    relox,
    ybuf,
    xbuf,
    tab,
    lenb,
    zbuf,
    ss,
    sx,
    rs,
    rx,
    so,
    sox,
    ro,
    rox,
    rr,
    rrx,
    fs,
    fsx,
    rro,
    rrox,
    fso,
    fsox,
    ysend,
    yrecv,
    xsend,
    xrecv,
    loc,
):
    cl = lax.axis_index("clip")
    i = lax.axis_index("seq")
    z = i // 2
    c = i % 2
    y = cl % ny
    x = cl // ny
    has_x = (c == 0) & (z % 3 != 0) & (i < 14)
    slot = z // 2
    relayed = (z == 0) | (z == 2) | (z == 5)
    my_e = z - 1 - z // 3

    def chip_at(t):
        mag = (4 - t // 2) * ((t + 7) // 8)
        return (z + mag * (1 - 2 * (t % 2)) + 8) % 8

    def rcopy(src, dst, send, recv, j):
        return pltpu.make_async_remote_copy(
            src, dst, send, recv, device_id={"seq": j}, device_id_type=MESH
        )

    def arrived(view, sem):
        pltpu.make_async_copy(view, view, sem).wait()

    def rows_of(j, n=TOK):
        return pl.ds(pl.multiple_of(j * n, n), n)

    def cols(start, n):
        return pl.ds(pl.multiple_of(start, 128), n)

    barrier = pltpu.get_barrier_semaphore()

    def greet(axis, j):
        pl.semaphore_signal(barrier, inc=1, device_id={axis: j}, device_id_type=MESH)

    for dy in range(1, ny):
        greet("clip", x * ny + (y + dy) % ny)
    for dx in range(1, nx):
        greet("clip", ((x + dx) % nx) * ny + y)
    near = ny - 1 + nx - 1

    def one(n, carry):
        @pl.when((n != i) & ((n < 14) | (i < 14)))
        def _():
            greet("seq", n)

        return carry

    lax.fori_loop(0, 16, one, 0)
    pl.semaphore_wait(barrier, near + 15 - i // 14)

    lane = lax.broadcasted_iota(jnp.int32, (8, 128), 1)
    mine = jnp.zeros((8, 128), jnp.int32)
    for m in range(4):
        mine = jnp.where(lane == 4 * cl + m, counts[m], mine)
    ybuf[y] = mine

    def ycopy(dy):
        return pltpu.make_async_remote_copy(
            ybuf.at[y],
            ybuf.at[y],
            ysend.at[dy],
            yrecv.at[y],
            device_id={"clip": x * ny + (y + dy) % ny},
            device_id_type=MESH,
        )

    def xcopy(dx):
        return pltpu.make_async_remote_copy(
            xbuf.at[x],
            xbuf.at[x],
            xsend.at[dx],
            xrecv.at[x],
            device_id={"clip": ((x + dx) % nx) * ny + y},
            device_id_type=MESH,
        )

    for dy in range(1, ny):
        ycopy(dy).start()

    arrays = ((k, kb, kx), (v, vb, vx), (q, qb, qx))

    def each_send(a, act):
        src, buf, bx = arrays[a]

        def one(tt, carry):
            t = (tt + 1) % 8
            w = chip_at(t)
            e = w - 1 - w // 3
            via = (t == 1) & relayed

            @pl.when(w != 7)
            def _():
                for cc in (0, 1):
                    j = 2 * w + cc
                    piece = src.at[0, :, cols(256 * j, 256)]

                    @pl.when(via)
                    def _():
                        act(rcopy(piece, rel.at[a, slot, cc], ss.at[a, j], rr.at[a, slot, cc], 14 + c))

                    @pl.when((j != i) & jnp.logical_not(via))
                    def _():
                        act(rcopy(piece, buf.at[rows_of(i)], ss.at[a, j], rs.at[a, i], j))

                @pl.when(w % 3 != 0)
                def _():
                    piece = src.at[0, :, cols(EXTRA0 + 128 * e, 128)]

                    @pl.when(via)
                    def _():
                        act(rcopy(piece, relx.at[a, slot], sx.at[a, e], rrx.at[a, slot], 14 + c))

                    @pl.when((2 * w != i) & jnp.logical_not(via))
                    def _():
                        act(rcopy(piece, bx.at[rows_of(i)], sx.at[a, e], rx.at[a, i], 2 * w))

            return carry

        lax.fori_loop(0, 8, one, 0)

    def own_copy(a):
        src, buf, bx = arrays[a]
        pltpu.make_async_copy(
            src.at[0, :, cols(256 * i, 256)], buf.at[rows_of(i)], rs.at[a, i]
        ).start()

        @pl.when(has_x)
        def _():
            pltpu.make_async_copy(
                src.at[0, :, cols(EXTRA0 + 128 * my_e, 128)], bx.at[rows_of(i)], rx.at[a, i]
            ).start()

    def await_block(a, w):
        _, buf, bx = arrays[a]
        for cc in (0, 1):
            j = 2 * w + cc
            arrived(buf.at[rows_of(j)], rs.at[a, j])

            @pl.when(has_x)
            def _():
                arrived(bx.at[rows_of(j)], rx.at[a, j])

    def turn(block, w):
        part = pl.ds(pl.multiple_of(w * WIDE, WIDE), WIDE)
        return block * tab[0, part] + pltpu.roll(block, HD // 2, 1) * tab[1, part]

    def positions(shape, dim):
        return lax.broadcasted_iota(jnp.int32, shape, dim).astype(F32)

    def start(copy):
        copy.start()

    def each_result(w, t, act):
        via = (t == 1) & relayed
        for cc in (0, 1):
            j = 2 * w + cc
            rows = rows_of(j)

            @pl.when(via)
            def _():
                act(rcopy(ob.at[rows], relo.at[slot, cc], so.at[j], rro.at[slot, cc], 14 + c))

                @pl.when(has_x)
                def _():
                    act(rcopy(ox.at[rows], relox.at[slot, cc], sox.at[j], rrox.at[slot, cc], 14 + c))

            @pl.when((j != i) & jnp.logical_not(via))
            def _():
                act(rcopy(ob.at[rows], out.at[0, :, cols(256 * i, 256)], so.at[j], ro.at[i], j))

                @pl.when(has_x)
                def _():
                    act(
                        rcopy(
                            ox.at[rows],
                            out.at[0, :, cols(EXTRA0 + 128 * my_e, 128)],
                            sox.at[j],
                            rox.at[my_e],
                            j,
                        )
                    )

    def gate_of(head):
        fraction = jnp.full((1, HD), timesteps[0], jnp.int32).astype(F32) / 1000.0
        sigma = 5.0 * fraction / (1.0 + 4.0 * fraction)
        return 1.0 + sigma * gain[pl.ds(head, 1), :]

    def attend(h, block, w, head):
        q_rot = turn(block.astype(F32), w).astype(BF)
        top = None
        for n in range(LIVE // WIDE):
            part = pl.ds(n * WIDE, WIDE)
            s = lax.dot_general(
                kr[h, part], q_rot, (((1,), (1,)), ((), ())), preferred_element_type=F32
            )
            sbuf[h, part] = s
            high = jnp.max(s.reshape(WIDE // 8, 8, WIDE), axis=0)
            top = high if top is None else jnp.maximum(top, high)
        top = jnp.max(top, axis=0, keepdims=True)
        total = None
        for n in range(LIVE // WIDE):
            part = pl.ds(n * WIDE, WIDE)
            p = jnp.exp2((sbuf[h, part] - top) * EXP_SCALE).astype(BF)
            term = jnp.dot(vt[h, :, part], p, preferred_element_type=F32)
            total = term if total is None else total + term
        mixed = total[:HD] * (1.0 / total[HD : HD + 1])
        mixed = jnp.transpose(mixed).astype(BF).astype(F32)
        pos = positions((WIDE, HD), 0) + (w * WIDE).astype(F32)
        return jnp.where(pos < lenb[0:1, 0:HD], mixed * gate_of(head), 0.0).astype(BF)

    @pl.when(i < 14)
    def _():
        table_copy = pltpu.make_async_copy(table, tab, loc.at[0])
        table_copy.start()
        for a in range(3):
            each_send(a, start)
            own_copy(a)
        table_copy.wait()

        def k_step(tt, carry):
            w = chip_at((8 - tt) % 8)

            @pl.when(w != 7)
            def _():
                part = pl.ds(pl.multiple_of(w * WIDE, WIDE), WIDE)
                await_block(0, w)
                for h in (0, 1):
                    kr[h, part] = turn(kb[part, h * HD : (h + 1) * HD].astype(F32), w).astype(BF)

                @pl.when(has_x)
                def _():
                    kr[2, part] = turn(kx[part].astype(F32), w).astype(BF)

            return carry

        lax.fori_loop(0, 8, k_step, 0)

    def source_of(n):
        return 2 * n + n // 2

    def forward(a, n, act, wait):
        _, buf, bx = arrays[a]
        o = source_of(n)
        w = (o + 4) % 8
        rows = rows_of(2 * o + c)
        for cc in (0, 1):
            if wait:
                arrived(rel.at[a, n, cc], rr.at[a, n, cc])
            act(rcopy(rel.at[a, n, cc], buf.at[rows], fs.at[a, n, cc], rs.at[a, 2 * o + c], 2 * w + cc))

        @pl.when(w % 3 != 0)
        def _():
            if wait:
                arrived(relx.at[a, n], rrx.at[a, n])
            act(rcopy(relx.at[a, n], bx.at[rows], fsx.at[a, n], rx.at[a, 2 * o + c], 2 * w))

    def relay(a):
        def pass_on(n, carry):
            forward(a, n, start, True)
            return carry

        lax.fori_loop(0, 3, pass_on, 0)

    @pl.when(i >= 14)
    def _():
        relay(0)

    for dy in range(1, ny):
        o = (y + dy) % ny
        arrived(ybuf.at[o], yrecv.at[o])
    xbuf[x] = jnp.sum(ybuf[...], axis=0)
    for dx in range(1, nx):
        xcopy(dx).start()
    for dx in range(1, nx):
        o = (x + dx) % nx
        arrived(xbuf.at[o], xrecv.at[o])
    pool = jnp.sum(xbuf[...], axis=0)
    picked = jnp.where(lane == assignment[0], pool, 0).astype(F32)
    length = jnp.sum(picked, axis=1, keepdims=True) * float(FRAME_TOK)
    lenb[...] = jnp.broadcast_to(length, (8, WIDE))
    for dy in range(1, ny):
        ycopy(dy).wait_send()
    for dx in range(1, nx):
        xcopy(dx).wait_send()

    @pl.when(i < 14)
    def _():
        for n in range(1, 4):
            part = pl.ds(n * FRAME_TOK, FRAME_TOK)
            live = positions((FRAME_TOK, HD), 0) + float(n * FRAME_TOK) < lenb[0:1, 0:HD]
            for h in range(3):

                def patch(h=h):
                    first = kr[h, 0:16].astype(F32)[0:1]
                    kr[h, part] = jnp.where(live, kr[h, part].astype(F32), first).astype(BF)

                if h < 2:
                    patch()
                else:
                    pl.when(has_x)(patch)

        def v_step(tt, carry):
            w = chip_at((8 - tt) % 8)

            @pl.when(w != 7)
            def _():
                part = pl.ds(pl.multiple_of(w * WIDE, WIDE), WIDE)
                await_block(1, w)
                pos = positions((1, WIDE), 1) + (w * WIDE).astype(F32)
                live = pos < lenb[0:1]
                ones = jnp.broadcast_to(jnp.where(live, 1.0, 0.0), (16, WIDE)).astype(BF)

                def put(h, block):
                    turned = jnp.transpose(block.astype(F32))
                    vt[h, 0:HD, part] = jnp.where(live, turned, 0.0).astype(BF)
                    vt[h, HD : HD + 16, part] = ones

                for h in (0, 1):
                    put(h, vb[part, h * HD : (h + 1) * HD])

                @pl.when(has_x)
                def _():
                    put(2, vx[part])

            return carry

        lax.fori_loop(0, 8, v_step, 0)

        def q_step(tt, carry):
            t = ((tt % 7) + 1) * ((tt + 6) // 7)
            w = chip_at(t)

            @pl.when(w != 7)
            def _():
                part = pl.ds(pl.multiple_of(w * WIDE, WIDE), WIDE)
                await_block(2, w)
                for h in (0, 1):
                    lanes = slice(h * HD, (h + 1) * HD)
                    ob[part, lanes] = attend(h, qb[part, lanes], w, 2 * i + h)

                @pl.when(has_x)
                def _():
                    ox[part] = attend(2, qx[part], w, 28 + my_e)

                each_result(w, t, start)

            return carry

        lax.fori_loop(0, 8, q_step, 0)

        own = [pltpu.make_async_copy(ob.at[rows_of(i)], out.at[0, :, cols(256 * i, 256)], loc.at[1])]
        own[0].start()
        own_x = pltpu.make_async_copy(
            ox.at[rows_of(i)], out.at[0, :, cols(EXTRA0 + 128 * my_e, 128)], loc.at[2]
        )

        @pl.when(has_x)
        def _():
            own_x.start()

        for a in range(3):
            each_send(a, lambda copy: copy.wait_send())

        def drain(t, carry):
            w = chip_at(t)

            @pl.when(w != 7)
            def _():
                each_result(w, t, lambda copy: copy.wait_send())

            return carry

        lax.fori_loop(0, 8, drain, 0)
        own[0].wait()

        @pl.when(has_x)
        def _():
            own_x.wait()

        def gather(j, carry):
            @pl.when(j != i)
            def _():
                arrived(out.at[0, :, cols(256 * j, 256)], ro.at[j])

            return carry

        lax.fori_loop(0, 14, gather, 0)

        def gather_x(e, carry):
            @pl.when(jnp.logical_not(has_x & (e == my_e)))
            def _():
                arrived(out.at[0, :, cols(EXTRA0 + 128 * e, 128)], rox.at[e])

            return carry

        lax.fori_loop(0, 4, gather_x, 0)

    @pl.when(i >= 14)
    def _():
        relay(1)
        relay(2)
        zbuf[...] = jnp.zeros_like(zbuf)
        blank = [
            pltpu.make_async_copy(zbuf, out.at[0, n * 16 : (n + 1) * 16], loc.at[n])
            for n in range(8)
        ]
        for copy in blank:
            copy.start()

        def forward_result(n, cc, act, wait):
            o = source_of(n)
            w = (o + 4) % 8
            j = 2 * o + c
            e = o - 1 - o // 3
            if wait:
                arrived(relo.at[n, cc], rro.at[n, cc])
            act(
                rcopy(
                    relo.at[n, cc], out.at[0, :, cols(256 * j, 256)], fso.at[n, cc], ro.at[j], 2 * w + cc
                )
            )

            @pl.when((o % 3 != 0) & (c == 0))
            def _():
                if wait:
                    arrived(relox.at[n, cc], rrox.at[n, cc])
                act(
                    rcopy(
                        relox.at[n, cc],
                        out.at[0, :, cols(EXTRA0 + 128 * e, 128)],
                        fsox.at[n, cc],
                        rox.at[e],
                        2 * w + cc,
                    )
                )

        def pass_result(n, carry):
            for cc in (0, 1):
                forward_result(n, cc, start, True)
            return carry

        lax.fori_loop(0, 3, pass_result, 0)

        def finish(n, carry):
            for a in range(3):
                forward(a, n, lambda copy: copy.wait_send(), False)
            for cc in (0, 1):
                forward_result(n, cc, lambda copy: copy.wait_send(), False)
            return carry

        lax.fori_loop(0, 3, finish, 0)
        for copy in blank:
            copy.wait()


def build(mesh):
    clips = mesh.shape["clip"]
    ny = min(8, clips)
    nx = clips // ny
    dma = pltpu.SemaphoreType.DMA

    def local(queries, keys, values, frame_counts, assignment, timesteps, gate_gain):
        def call(*args):
            kernel(nx, ny, *args)

        anywhere = pl.BlockSpec(memory_space=pl.ANY)
        scalars = pl.BlockSpec(memory_space=pltpu.SMEM)
        return pl.pallas_call(
            call,
            out_shape=jax.ShapeDtypeStruct(queries.shape, BF),
            in_specs=[anywhere] * 3
            + [scalars] * 3
            + [pl.BlockSpec(memory_space=pltpu.VMEM), anywhere],
            out_specs=anywhere,
            scratch_shapes=[pltpu.VMEM((LIVE, 256), BF)] * 4
            + [pltpu.VMEM((LIVE, HD), BF)] * 4
            + [
                pltpu.VMEM((3, LIVE, HD), BF),
                pltpu.VMEM((3, HD + 16, LIVE), BF),
                pltpu.VMEM((3, LIVE, WIDE), F32),
                pltpu.VMEM((3, 3, 2, TOK, 256), BF),
                pltpu.VMEM((3, 3, TOK, HD), BF),
                pltpu.VMEM((3, 2, TOK, 256), BF),
                pltpu.VMEM((3, 2, TOK, HD), BF),
                pltpu.VMEM((ny, 8, 128), jnp.int32),
                pltpu.VMEM((nx, 8, 128), jnp.int32),
                pltpu.VMEM((2, LIVE, HD), F32),
                pltpu.VMEM((8, WIDE), F32),
                pltpu.VMEM((16, 4096), BF),
                dma((3, 14)),
                dma((3, 4)),
                dma((3, 14)),
                dma((3, 14)),
                dma((14,)),
                dma((14,)),
                dma((14,)),
                dma((4,)),
                dma((3, 3, 2)),
                dma((3, 3)),
                dma((3, 3, 2)),
                dma((3, 3)),
                dma((3, 2)),
                dma((3, 2)),
                dma((3, 2)),
                dma((3, 2)),
                dma((8,)),
                dma((8,)),
                dma((4,)),
                dma((4,)),
                dma((8,)),
            ],
            compiler_params=pltpu.CompilerParams(
                collective_id=0, has_side_effects=True, vmem_limit_bytes=63 * 2**20
            ),
            cost_estimate=pl.CostEstimate(
                flops=4 * 1792 * 1792 * 256,
                bytes_accessed=8 * 2**20,
                transcendentals=2 * 1792 * 1792,
            ),
        )(
            queries,
            keys,
            values,
            frame_counts,
            assignment,
            timesteps,
            gate_gain.reshape(32, HD),
            jnp.asarray(rope_tables()),
        )

    tokens = P("clip", "seq", None)
    return jax.shard_map(
        local,
        mesh=mesh,
        in_specs=(tokens, tokens, tokens, P("clip"), P("clip"), P("clip"), P()),
        out_specs=tokens,
        check_vma=False,
    )


def solution(mesh):
    return build(mesh)
```

```python
import math

import jax
import jax.numpy as jnp
import numpy as np
from jax import lax
from jax.experimental import pallas as pl
from jax.experimental.pallas import tpu as pltpu
from jax.sharding import PartitionSpec as P

HD = 128
FRAME_TOK = 448
GRID_W = 28
LIVE = 1792
TOK = 128
EXTRA0 = 3584
COUNTER = 14
RELAY = 15
MESH = pl.DeviceIdType.MESH
EXP_SCALE = HD ** (-0.5) * math.log2(math.e)
BF = jnp.bfloat16
F32 = jnp.float32
WIDE = 256


def rope_tables():
    position = np.arange(LIVE)
    frame = (position // FRAME_TOK).astype(np.float32)
    within = position % FRAME_TOK
    row_pos = (within // GRID_W).astype(np.float32)
    col_pos = (within % GRID_W).astype(np.float32)
    inv_time = 10000.0 ** (-2.0 * np.arange(22) / 44.0)
    inv_space = 10000.0 ** (-2.0 * np.arange(21) / 42.0)
    angles = np.concatenate(
        [
            frame[:, None] * inv_time[None, :],
            row_pos[:, None] * inv_space[None, :],
            col_pos[:, None] * inv_space[None, :],
        ],
        axis=1,
    )
    cosine, sine = np.cos(angles), np.sin(angles)
    table = np.stack(
        [np.concatenate([cosine, cosine], axis=1), np.concatenate([-sine, sine], axis=1)]
    )
    return table.astype(np.float32)


def kernel(
    nx,
    ny,
    q,
    k,
    v,
    counts,
    assignment,
    timesteps,
    gain,
    table,
    out,
    qb,
    kb,
    vb,
    ob,
    qx,
    kx,
    vx,
    ox,
    kr,
    vt,
    sbuf,
    rel,
    relx,
    relo,
    relox,
    ybuf,
    xbuf,
    tab,
    lenb,
    zbuf,
    ss,
    sx,
    rs,
    rx,
    so,
    sox,
    ro,
    rox,
    rr,
    rrx,
    fs,
    fsx,
    rro,
    rrox,
    fso,
    fsox,
    ysend,
    yrecv,
    xsend,
    xrecv,
    loc,
    lsend,
    lrecv,
    ready,
):
    cl = lax.axis_index("clip")
    i = lax.axis_index("seq")
    z = i // 2
    c = i % 2
    y = cl % ny
    x = cl // ny
    has_x = (c == 0) & (z % 3 != 0) & (i < 14)
    slot = z // 2
    relayed = (z == 0) | (z == 2) | (z == 5)
    my_e = z - 1 - z // 3

    def chip_at(t):
        mag = (4 - t // 2) * ((t + 7) // 8)
        return (z + mag * (1 - 2 * (t % 2)) + 8) % 8

    def rcopy(src, dst, send, recv, j):
        return pltpu.make_async_remote_copy(
            src, dst, send, recv, device_id={"seq": j}, device_id_type=MESH
        )

    def arrived(view, sem):
        pltpu.make_async_copy(view, view, sem).wait()

    def rows_of(j, n=TOK):
        return pl.ds(pl.multiple_of(j * n, n), n)

    def cols(start, n):
        return pl.ds(pl.multiple_of(start, 128), n)

    barrier = pltpu.get_barrier_semaphore()

    def greet(axis, j):
        pl.semaphore_signal(barrier, inc=1, device_id={axis: j}, device_id_type=MESH)

    def tell(j):
        pl.semaphore_signal(ready.at[i], inc=1, device_id={"seq": j}, device_id_type=MESH)

    near = ny - 1 + nx - 1

    @pl.when(i == COUNTER)
    def _():
        for dy in range(1, ny):
            greet("clip", x * ny + (y + dy) % ny)
        for dx in range(1, nx):
            greet("clip", ((x + dx) % nx) * ny + y)

    @pl.when(i < 14)
    def _():
        def one(n, carry):
            @pl.when(n > i)
            def _():
                greet("seq", n)

            return carry

        lax.fori_loop(0, 16, one, 0)

        @pl.when(i > 0)
        def _():
            pl.semaphore_wait(barrier, i)

        def back(n, carry):
            @pl.when(n < i)
            def _():
                tell(n)

            return carry

        lax.fori_loop(0, 14, back, 0)

    @pl.when(i == COUNTER)
    def _():
        pl.semaphore_wait(barrier, 14 + near)

    @pl.when(i == RELAY)
    def _():
        pl.semaphore_wait(barrier, 14)
        for o in (0, 2, 5):
            for cc in (0, 1):
                tell(2 * o + cc)

    arrays = ((k, kb, kx), (v, vb, vx), (q, qb, qx))

    def each_send(a, act, first=False):
        src, buf, bx = arrays[a]

        def one(tt, carry):
            below = (8 + z - tt) // 8
            w = below * (z - tt) + (1 - below) * tt if first else chip_at((tt + 1) % 8)
            e = w - 1 - w // 3
            via = (w == (z + 4) % 8) & relayed

            @pl.when(w != 7)
            def _():
                for cc in (0, 1):
                    j = 2 * w + cc
                    piece = src.at[0, :, cols(256 * j, 256)]
                    if first:

                        @pl.when(j > i)
                        def _():
                            pl.semaphore_wait(ready.at[j], 1)

                        if cc == 0:

                            @pl.when(via)
                            def _():
                                pl.semaphore_wait(ready.at[RELAY], 1)

                    @pl.when(via)
                    def _():
                        act(rcopy(piece, rel.at[a, slot, c, cc], ss.at[a, j], rr.at[a, slot, c, cc], RELAY))

                    @pl.when((j != i) & jnp.logical_not(via))
                    def _():
                        act(rcopy(piece, buf.at[rows_of(i)], ss.at[a, j], rs.at[a, i], j))

                @pl.when(w % 3 != 0)
                def _():
                    piece = src.at[0, :, cols(EXTRA0 + 128 * e, 128)]

                    @pl.when(via)
                    def _():
                        act(rcopy(piece, relx.at[a, slot, c], sx.at[a, e], rrx.at[a, slot, c], RELAY))

                    @pl.when((2 * w != i) & jnp.logical_not(via))
                    def _():
                        act(rcopy(piece, bx.at[rows_of(i)], sx.at[a, e], rx.at[a, i], 2 * w))

            return carry

        lax.fori_loop(0, 8, one, 0)

    def own_copy(a):
        src, buf, bx = arrays[a]
        pltpu.make_async_copy(
            src.at[0, :, cols(256 * i, 256)], buf.at[rows_of(i)], rs.at[a, i]
        ).start()

        @pl.when(has_x)
        def _():
            pltpu.make_async_copy(
                src.at[0, :, cols(EXTRA0 + 128 * my_e, 128)], bx.at[rows_of(i)], rx.at[a, i]
            ).start()

    def await_block(a, w):
        _, buf, bx = arrays[a]
        for cc in (0, 1):
            j = 2 * w + cc
            arrived(buf.at[rows_of(j)], rs.at[a, j])

            @pl.when(has_x)
            def _():
                arrived(bx.at[rows_of(j)], rx.at[a, j])

    def turn(block, w):
        part = pl.ds(pl.multiple_of(w * WIDE, WIDE), WIDE)
        return block * tab[0, part] + pltpu.roll(block, HD // 2, 1) * tab[1, part]

    def positions(shape, dim):
        return lax.broadcasted_iota(jnp.int32, shape, dim).astype(F32)

    def start(copy):
        copy.start()

    def each_result(w, t, act):
        via = (t == 1) & relayed
        for cc in (0, 1):
            j = 2 * w + cc
            rows = rows_of(j)

            @pl.when(via)
            def _():
                act(rcopy(ob.at[rows], relo.at[slot, c, cc], so.at[j], rro.at[slot, c, cc], RELAY))

                @pl.when(has_x)
                def _():
                    act(rcopy(ox.at[rows], relox.at[slot, cc], sox.at[j], rrox.at[slot, cc], RELAY))

            @pl.when((j != i) & jnp.logical_not(via))
            def _():
                act(rcopy(ob.at[rows], out.at[0, :, cols(256 * i, 256)], so.at[j], ro.at[i], j))

                @pl.when(has_x)
                def _():
                    act(
                        rcopy(
                            ox.at[rows],
                            out.at[0, :, cols(EXTRA0 + 128 * my_e, 128)],
                            sox.at[j],
                            rox.at[my_e],
                            j,
                        )
                    )

    def gate_of(head):
        fraction = jnp.full((1, HD), timesteps[0], jnp.int32).astype(F32) / 1000.0
        sigma = 5.0 * fraction / (1.0 + 4.0 * fraction)
        return 1.0 + sigma * gain[pl.ds(head, 1), :]

    def attend(h, block, w, head):
        q_rot = turn(block.astype(F32), w).astype(BF)
        top = None
        for n in range(LIVE // WIDE):
            part = pl.ds(n * WIDE, WIDE)
            s = lax.dot_general(
                kr[h, part], q_rot, (((1,), (1,)), ((), ())), preferred_element_type=F32
            )
            sbuf[h, part] = s
            high = jnp.max(s.reshape(WIDE // 8, 8, WIDE), axis=0)
            top = high if top is None else jnp.maximum(top, high)
        top = jnp.max(top, axis=0, keepdims=True)
        total = None
        for n in range(LIVE // WIDE):
            part = pl.ds(n * WIDE, WIDE)
            p = jnp.exp2((sbuf[h, part] - top) * EXP_SCALE).astype(BF)
            term = jnp.dot(vt[h, :, part], p, preferred_element_type=F32)
            total = term if total is None else total + term
        mixed = total[:HD] * (1.0 / total[HD : HD + 1])
        mixed = jnp.transpose(mixed).astype(BF).astype(F32)
        pos = positions((WIDE, HD), 0) + (w * WIDE).astype(F32)
        return jnp.where(pos < lenb[0:1, 0:HD], mixed * gate_of(head), 0.0).astype(BF)

    @pl.when(i < 14)
    def _():
        table_copy = pltpu.make_async_copy(table, tab, loc.at[0])
        table_copy.start()
        for a in range(3):
            each_send(a, start, a == 0)
            own_copy(a)
        table_copy.wait()

        def k_step(tt, carry):
            w = chip_at((8 - tt) % 8)

            @pl.when(w != 7)
            def _():
                part = pl.ds(pl.multiple_of(w * WIDE, WIDE), WIDE)
                await_block(0, w)
                for h in (0, 1):
                    kr[h, part] = turn(kb[part, h * HD : (h + 1) * HD].astype(F32), w).astype(BF)

                @pl.when(has_x)
                def _():
                    kr[2, part] = turn(kx[part].astype(F32), w).astype(BF)

            return carry

        lax.fori_loop(0, 8, k_step, 0)

    def source_of(n):
        return 2 * n + n // 2

    def forward(a, n, act, wait):
        _, buf, bx = arrays[a]
        o = source_of(n)
        w = (o + 4) % 8
        for oc in (0, 1):
            j = 2 * o + oc
            for cc in (0, 1):
                if wait:
                    arrived(rel.at[a, n, oc, cc], rr.at[a, n, oc, cc])
                act(
                    rcopy(
                        rel.at[a, n, oc, cc], buf.at[rows_of(j)], fs.at[a, n, oc, cc], rs.at[a, j], 2 * w + cc
                    )
                )

            @pl.when(w % 3 != 0)
            def _():
                if wait:
                    arrived(relx.at[a, n, oc], rrx.at[a, n, oc])
                act(rcopy(relx.at[a, n, oc], bx.at[rows_of(j)], fsx.at[a, n, oc], rx.at[a, j], 2 * w))

    def relay(a):
        def pass_on(n, carry):
            forward(a, n, start, True)
            return carry

        lax.fori_loop(0, 3, pass_on, 0)

    @pl.when(i == RELAY)
    def _():
        relay(0)
        relay(1)
        relay(2)

    @pl.when(i == COUNTER)
    def _():
        lane = lax.broadcasted_iota(jnp.int32, (8, 128), 1)
        mine = jnp.zeros((8, 128), jnp.int32)
        for m in range(4):
            mine = jnp.where(lane == 4 * cl + m, counts[m], mine)
        ybuf[y] = mine

        def ycopy(dy):
            return pltpu.make_async_remote_copy(
                ybuf.at[y],
                ybuf.at[y],
                ysend.at[dy],
                yrecv.at[y],
                device_id={"clip": x * ny + (y + dy) % ny},
                device_id_type=MESH,
            )

        def xcopy(dx):
            return pltpu.make_async_remote_copy(
                xbuf.at[x],
                xbuf.at[x],
                xsend.at[dx],
                xrecv.at[x],
                device_id={"clip": ((x + dx) % nx) * ny + y},
                device_id_type=MESH,
            )

        for dy in range(1, ny):
            ycopy(dy).start()
        for dy in range(1, ny):
            o = (y + dy) % ny
            arrived(ybuf.at[o], yrecv.at[o])
        xbuf[x] = jnp.sum(ybuf[...], axis=0)
        for dx in range(1, nx):
            xcopy(dx).start()
        for dx in range(1, nx):
            o = (x + dx) % nx
            arrived(xbuf.at[o], xrecv.at[o])
        pool = jnp.sum(xbuf[...], axis=0)
        picked = jnp.where(lane == assignment[0], pool, 0).astype(F32)
        length = jnp.sum(picked, axis=1, keepdims=True) * float(FRAME_TOK)
        lenb[...] = jnp.broadcast_to(length, (8, WIDE))

        def publish(n, carry):
            rcopy(lenb, lenb, lsend.at[n], lrecv.at[0], n).start()
            return carry

        lax.fori_loop(0, 14, publish, 0)
        for dy in range(1, ny):
            ycopy(dy).wait_send()
        for dx in range(1, nx):
            xcopy(dx).wait_send()

        def published(n, carry):
            rcopy(lenb, lenb, lsend.at[n], lrecv.at[0], n).wait_send()
            return carry

        lax.fori_loop(0, 14, published, 0)

    @pl.when(i < 14)
    def _():
        arrived(lenb, lrecv.at[0])
        for n in range(1, 4):
            part = pl.ds(n * FRAME_TOK, FRAME_TOK)
            live = positions((FRAME_TOK, HD), 0) + float(n * FRAME_TOK) < lenb[0:1, 0:HD]
            for h in range(3):

                def patch(h=h):
                    first = kr[h, 0:16].astype(F32)[0:1]
                    kr[h, part] = jnp.where(live, kr[h, part].astype(F32), first).astype(BF)

                if h < 2:
                    patch()
                else:
                    pl.when(has_x)(patch)

        def v_step(tt, carry):
            w = chip_at((8 - tt) % 8)

            @pl.when(w != 7)
            def _():
                part = pl.ds(pl.multiple_of(w * WIDE, WIDE), WIDE)
                await_block(1, w)
                pos = positions((1, WIDE), 1) + (w * WIDE).astype(F32)
                live = pos < lenb[0:1]
                ones = jnp.broadcast_to(jnp.where(live, 1.0, 0.0), (16, WIDE)).astype(BF)

                def put(h, block):
                    turned = jnp.transpose(block.astype(F32))
                    vt[h, 0:HD, part] = jnp.where(live, turned, 0.0).astype(BF)
                    vt[h, HD : HD + 16, part] = ones

                for h in (0, 1):
                    put(h, vb[part, h * HD : (h + 1) * HD])

                @pl.when(has_x)
                def _():
                    put(2, vx[part])

            return carry

        lax.fori_loop(0, 8, v_step, 0)

        def q_step(tt, carry):
            perm = [0, 2, 3, 1, 4, 5, 6, 7]
            t = perm[7]
            for step in range(7):
                t = jnp.where(tt == step, perm[step], t)
            w = chip_at(t)

            @pl.when(w != 7)
            def _():
                part = pl.ds(pl.multiple_of(w * WIDE, WIDE), WIDE)
                await_block(2, w)
                for h in (0, 1):
                    lanes = slice(h * HD, (h + 1) * HD)
                    ob[part, lanes] = attend(h, qb[part, lanes], w, 2 * i + h)

                @pl.when(has_x)
                def _():
                    ox[part] = attend(2, qx[part], w, 28 + my_e)

                each_result(w, t, start)

            return carry

        lax.fori_loop(0, 8, q_step, 0)

        own = [pltpu.make_async_copy(ob.at[rows_of(i)], out.at[0, :, cols(256 * i, 256)], loc.at[1])]
        own[0].start()
        own_x = pltpu.make_async_copy(
            ox.at[rows_of(i)], out.at[0, :, cols(EXTRA0 + 128 * my_e, 128)], loc.at[2]
        )

        @pl.when(has_x)
        def _():
            own_x.start()

        for a in range(3):
            each_send(a, lambda copy: copy.wait_send())

        def drain(t, carry):
            w = chip_at(t)

            @pl.when(w != 7)
            def _():
                each_result(w, t, lambda copy: copy.wait_send())

            return carry

        lax.fori_loop(0, 8, drain, 0)
        own[0].wait()

        @pl.when(has_x)
        def _():
            own_x.wait()

        def gather(j, carry):
            @pl.when(j != i)
            def _():
                arrived(out.at[0, :, cols(256 * j, 256)], ro.at[j])

            return carry

        lax.fori_loop(0, 14, gather, 0)

        def gather_x(e, carry):
            @pl.when(jnp.logical_not(has_x & (e == my_e)))
            def _():
                arrived(out.at[0, :, cols(EXTRA0 + 128 * e, 128)], rox.at[e])

            return carry

        lax.fori_loop(0, 4, gather_x, 0)

    @pl.when(i >= 14)
    def _():
        zbuf[...] = jnp.zeros_like(zbuf)
        blank = [
            pltpu.make_async_copy(zbuf, out.at[0, n * 16 : (n + 1) * 16], loc.at[n])
            for n in range(8)
        ]
        for copy in blank:
            copy.start()
        for copy in blank:
            copy.wait()

    @pl.when(i == RELAY)
    def _():
        def forward_result(n, act, wait):
            o = source_of(n)
            w = (o + 4) % 8
            e = o - 1 - o // 3
            for cc in (0, 1):
                for oc in (0, 1):
                    j = 2 * o + oc
                    if wait:
                        arrived(relo.at[n, oc, cc], rro.at[n, oc, cc])
                    act(
                        rcopy(
                            relo.at[n, oc, cc],
                            out.at[0, :, cols(256 * j, 256)],
                            fso.at[n, oc, cc],
                            ro.at[j],
                            2 * w + cc,
                        )
                    )

                @pl.when(o % 3 != 0)
                def _():
                    if wait:
                        arrived(relox.at[n, cc], rrox.at[n, cc])
                    act(
                        rcopy(
                            relox.at[n, cc],
                            out.at[0, :, cols(EXTRA0 + 128 * e, 128)],
                            fsox.at[n, cc],
                            rox.at[e],
                            2 * w + cc,
                        )
                    )

        def pass_result(n, carry):
            forward_result(n, start, True)
            return carry

        lax.fori_loop(0, 3, pass_result, 0)

        def finish(n, carry):
            for a in range(3):
                forward(a, n, lambda copy: copy.wait_send(), False)
            forward_result(n, lambda copy: copy.wait_send(), False)
            return carry

        lax.fori_loop(0, 3, finish, 0)


def build(mesh):
    clips = mesh.shape["clip"]
    ny = min(8, clips)
    nx = clips // ny
    dma = pltpu.SemaphoreType.DMA

    def local(queries, keys, values, frame_counts, assignment, timesteps, gate_gain):
        def call(*args):
            kernel(nx, ny, *args)

        anywhere = pl.BlockSpec(memory_space=pl.ANY)
        scalars = pl.BlockSpec(memory_space=pltpu.SMEM)
        return pl.pallas_call(
            call,
            out_shape=jax.ShapeDtypeStruct(queries.shape, BF),
            in_specs=[anywhere] * 3
            + [scalars] * 3
            + [pl.BlockSpec(memory_space=pltpu.VMEM), anywhere],
            out_specs=anywhere,
            scratch_shapes=[pltpu.VMEM((LIVE, 256), BF)] * 4
            + [pltpu.VMEM((LIVE, HD), BF)] * 4
            + [
                pltpu.VMEM((3, LIVE, HD), BF),
                pltpu.VMEM((3, HD + 16, LIVE), BF),
                pltpu.VMEM((3, LIVE, WIDE), F32),
                pltpu.VMEM((3, 3, 2, 2, TOK, 256), BF),
                pltpu.VMEM((3, 3, 2, TOK, HD), BF),
                pltpu.VMEM((3, 2, 2, TOK, 256), BF),
                pltpu.VMEM((3, 2, TOK, HD), BF),
                pltpu.VMEM((ny, 8, 128), jnp.int32),
                pltpu.VMEM((nx, 8, 128), jnp.int32),
                pltpu.VMEM((2, LIVE, HD), F32),
                pltpu.VMEM((8, WIDE), F32),
                pltpu.VMEM((16, 4096), BF),
                dma((3, 14)),
                dma((3, 4)),
                dma((3, 14)),
                dma((3, 14)),
                dma((14,)),
                dma((14,)),
                dma((14,)),
                dma((4,)),
                dma((3, 3, 2, 2)),
                dma((3, 3, 2)),
                dma((3, 3, 2, 2)),
                dma((3, 3, 2)),
                dma((3, 2, 2)),
                dma((3, 2)),
                dma((3, 2, 2)),
                dma((3, 2)),
                dma((8,)),
                dma((8,)),
                dma((4,)),
                dma((4,)),
                dma((8,)),
                dma((14,)),
                dma((1,)),
                pltpu.SemaphoreType.REGULAR((16,)),
            ],
            compiler_params=pltpu.CompilerParams(
                collective_id=0, has_side_effects=True, vmem_limit_bytes=63 * 2**20
            ),
            cost_estimate=pl.CostEstimate(
                flops=4 * 1792 * 1792 * 256,
                bytes_accessed=8 * 2**20,
                transcendentals=2 * 1792 * 1792,
            ),
        )(
            queries,
            keys,
            values,
            frame_counts,
            assignment,
            timesteps,
            gate_gain.reshape(32, HD),
            jnp.asarray(rope_tables()),
        )

    tokens = P("clip", "seq", None)
    return jax.shard_map(
        local,
        mesh=mesh,
        in_specs=(tokens, tokens, tokens, P("clip"), P("clip"), P("clip"), P()),
        out_specs=tokens,
        check_vma=False,
    )


def solution(mesh):
    return build(mesh)
```

```python
import math

import jax
import jax.numpy as jnp
import numpy as np
from jax import lax
from jax.experimental import pallas as pl
from jax.experimental.pallas import tpu as pltpu
from jax.sharding import PartitionSpec as P

HD = 128
FRAME_TOK = 448
GRID_W = 28
LIVE = 1792
TOK = 128
EXTRA0 = 3584
COUNTER = 14
RELAY = 15
MESH = pl.DeviceIdType.MESH
EXP_SCALE = HD ** (-0.5) * math.log2(math.e)
BF = jnp.bfloat16
F32 = jnp.float32
WIDE = 256


def rope_tables():
    position = np.arange(LIVE)
    frame = (position // FRAME_TOK).astype(np.float32)
    within = position % FRAME_TOK
    row_pos = (within // GRID_W).astype(np.float32)
    col_pos = (within % GRID_W).astype(np.float32)
    inv_time = 10000.0 ** (-2.0 * np.arange(22) / 44.0)
    inv_space = 10000.0 ** (-2.0 * np.arange(21) / 42.0)
    angles = np.concatenate(
        [
            frame[:, None] * inv_time[None, :],
            row_pos[:, None] * inv_space[None, :],
            col_pos[:, None] * inv_space[None, :],
        ],
        axis=1,
    )
    cosine, sine = np.cos(angles), np.sin(angles)
    table = np.stack(
        [np.concatenate([cosine, cosine], axis=1), np.concatenate([-sine, sine], axis=1)]
    )
    return table.astype(np.float32)


def kernel(
    nx,
    ny,
    q,
    k,
    v,
    counts,
    assignment,
    timesteps,
    gain,
    table,
    out,
    qb,
    kb,
    vb,
    ob,
    qx,
    kx,
    vx,
    ox,
    kr,
    vt,
    sbuf,
    rel,
    relx,
    relo,
    relox,
    ybuf,
    xbuf,
    tab,
    lenb,
    zbuf,
    ss,
    sx,
    rs,
    rx,
    so,
    sox,
    ro,
    rox,
    rr,
    rrx,
    fs,
    fsx,
    rro,
    rrox,
    fso,
    fsox,
    ysend,
    yrecv,
    xsend,
    xrecv,
    loc,
    lsend,
    lrecv,
    ready,
):
    cl = lax.axis_index("clip")
    i = lax.axis_index("seq")
    z = i // 2
    c = i % 2
    y = cl % ny
    x = cl // ny
    has_x = (c == 0) & (z % 3 != 0) & (i < 14)
    slot = z // 2
    relayed = (z == 0) | (z == 2) | (z == 5)
    my_e = z - 1 - z // 3

    def chip_at(t):
        mag = (4 - t // 2) * ((t + 7) // 8)
        return (z + mag * (1 - 2 * (t % 2)) + 8) % 8

    def rcopy(src, dst, send, recv, j):
        return pltpu.make_async_remote_copy(
            src, dst, send, recv, device_id={"seq": j}, device_id_type=MESH
        )

    def arrived(view, sem):
        pltpu.make_async_copy(view, view, sem).wait()

    def rows_of(j, n=TOK):
        return pl.ds(pl.multiple_of(j * n, n), n)

    def cols(start, n):
        return pl.ds(pl.multiple_of(start, 128), n)

    barrier = pltpu.get_barrier_semaphore()

    def greet(axis, j):
        pl.semaphore_signal(barrier, inc=1, device_id={axis: j}, device_id_type=MESH)

    def tell(j):
        pl.semaphore_signal(ready.at[i], inc=1, device_id={"seq": j}, device_id_type=MESH)

    near = ny - 1 + nx - 1

    @pl.when(i == COUNTER)
    def _():
        for dy in range(1, ny):
            greet("clip", x * ny + (y + dy) % ny)
        for dx in range(1, nx):
            greet("clip", ((x + dx) % nx) * ny + y)

    @pl.when(i < 14)
    def _():
        def one(n, carry):
            @pl.when(n > i)
            def _():
                greet("seq", n)

            return carry

        lax.fori_loop(0, 16, one, 0)

        @pl.when(i > 0)
        def _():
            pl.semaphore_wait(barrier, i)

        def back(n, carry):
            @pl.when(n < i)
            def _():
                tell(n)

            return carry

        lax.fori_loop(0, 14, back, 0)

    @pl.when(i == COUNTER)
    def _():
        pl.semaphore_wait(barrier, 14 + near)

    @pl.when(i == RELAY)
    def _():
        pl.semaphore_wait(barrier, 14)
        for o in (0, 2, 5):
            for cc in (0, 1):
                tell(2 * o + cc)

    arrays = ((k, kb, kx), (v, vb, vx), (q, qb, qx))

    def each_send(a, act, first=False):
        src, buf, bx = arrays[a]

        def one(tt, carry):
            w = chip_at((tt + 1) % 8)
            e = w - 1 - w // 3
            via = (w == (z + 4) % 8) & relayed

            @pl.when(w != 7)
            def _():
                for cc in (0, 1):
                    j = 2 * w + cc
                    piece = src.at[0, :, cols(256 * j, 256)]
                    if first:

                        @pl.when(j > i)
                        def _():
                            pl.semaphore_wait(ready.at[j], 1)

                        if cc == 0:

                            @pl.when(via)
                            def _():
                                pl.semaphore_wait(ready.at[RELAY], 1)

                    @pl.when(via)
                    def _():
                        act(rcopy(piece, rel.at[a, slot, c, cc], ss.at[a, j], rr.at[a, slot, c, cc], RELAY))

                    @pl.when((j != i) & jnp.logical_not(via))
                    def _():
                        act(rcopy(piece, buf.at[rows_of(i)], ss.at[a, j], rs.at[a, i], j))

                @pl.when(w % 3 != 0)
                def _():
                    piece = src.at[0, :, cols(EXTRA0 + 128 * e, 128)]

                    @pl.when(via)
                    def _():
                        act(rcopy(piece, relx.at[a, slot, c], sx.at[a, e], rrx.at[a, slot, c], RELAY))

                    @pl.when((2 * w != i) & jnp.logical_not(via))
                    def _():
                        act(rcopy(piece, bx.at[rows_of(i)], sx.at[a, e], rx.at[a, i], 2 * w))

            return carry

        lax.fori_loop(0, 8, one, 0)

    def own_copy(a):
        src, buf, bx = arrays[a]
        pltpu.make_async_copy(
            src.at[0, :, cols(256 * i, 256)], buf.at[rows_of(i)], rs.at[a, i]
        ).start()

        @pl.when(has_x)
        def _():
            pltpu.make_async_copy(
                src.at[0, :, cols(EXTRA0 + 128 * my_e, 128)], bx.at[rows_of(i)], rx.at[a, i]
            ).start()

    def await_block(a, w):
        _, buf, bx = arrays[a]
        for cc in (0, 1):
            j = 2 * w + cc
            arrived(buf.at[rows_of(j)], rs.at[a, j])

            @pl.when(has_x)
            def _():
                arrived(bx.at[rows_of(j)], rx.at[a, j])

    def turn(block, w):
        part = pl.ds(pl.multiple_of(w * WIDE, WIDE), WIDE)
        return block * tab[0, part] + pltpu.roll(block, HD // 2, 1) * tab[1, part]

    def positions(shape, dim):
        return lax.broadcasted_iota(jnp.int32, shape, dim).astype(F32)

    def start(copy):
        copy.start()

    def each_result(w, t, act):
        via = (t == 1) & relayed
        for cc in (0, 1):
            j = 2 * w + cc
            rows = rows_of(j)

            @pl.when(via)
            def _():
                act(rcopy(ob.at[rows], relo.at[slot, c, cc], so.at[j], rro.at[slot, c, cc], RELAY))

                @pl.when(has_x)
                def _():
                    act(rcopy(ox.at[rows], relox.at[slot, cc], sox.at[j], rrox.at[slot, cc], RELAY))

            @pl.when((j != i) & jnp.logical_not(via))
            def _():
                act(rcopy(ob.at[rows], out.at[0, :, cols(256 * i, 256)], so.at[j], ro.at[i], j))

                @pl.when(has_x)
                def _():
                    act(
                        rcopy(
                            ox.at[rows],
                            out.at[0, :, cols(EXTRA0 + 128 * my_e, 128)],
                            sox.at[j],
                            rox.at[my_e],
                            j,
                        )
                    )

    def gate_of(head):
        fraction = jnp.full((1, HD), timesteps[0], jnp.int32).astype(F32) / 1000.0
        sigma = 5.0 * fraction / (1.0 + 4.0 * fraction)
        return 1.0 + sigma * gain[pl.ds(head, 1), :]

    def attend(h, block, w, head):
        q_rot = turn(block.astype(F32), w).astype(BF)
        top = None
        for n in range(LIVE // WIDE):
            part = pl.ds(n * WIDE, WIDE)
            s = lax.dot_general(
                kr[h, part], q_rot, (((1,), (1,)), ((), ())), preferred_element_type=F32
            )
            sbuf[h, part] = s
            high = jnp.max(s.reshape(WIDE // 8, 8, WIDE), axis=0)
            top = high if top is None else jnp.maximum(top, high)
        top = jnp.max(top, axis=0, keepdims=True)
        total = None
        for n in range(LIVE // WIDE):
            part = pl.ds(n * WIDE, WIDE)
            p = jnp.exp2((sbuf[h, part] - top) * EXP_SCALE).astype(BF)
            term = jnp.dot(vt[h, :, part], p, preferred_element_type=F32)
            total = term if total is None else total + term
        mixed = total[:HD] * (1.0 / total[HD : HD + 1])
        mixed = jnp.transpose(mixed).astype(BF).astype(F32)
        pos = positions((WIDE, HD), 0) + (w * WIDE).astype(F32)
        return jnp.where(pos < lenb[0:1, 0:HD], mixed * gate_of(head), 0.0).astype(BF)

    @pl.when(i < 14)
    def _():
        table_copy = pltpu.make_async_copy(table, tab, loc.at[0])
        table_copy.start()
        for a in range(3):
            each_send(a, start, a == 0)
            own_copy(a)
        table_copy.wait()

        def k_step(tt, carry):
            w = chip_at((8 - tt) % 8)

            @pl.when(w != 7)
            def _():
                part = pl.ds(pl.multiple_of(w * WIDE, WIDE), WIDE)
                await_block(0, w)
                for h in (0, 1):
                    kr[h, part] = turn(kb[part, h * HD : (h + 1) * HD].astype(F32), w).astype(BF)

                @pl.when(has_x)
                def _():
                    kr[2, part] = turn(kx[part].astype(F32), w).astype(BF)

            return carry

        lax.fori_loop(0, 8, k_step, 0)

    def source_of(n):
        return 2 * n + n // 2

    def forward(a, n, act, wait):
        _, buf, bx = arrays[a]
        o = source_of(n)
        w = (o + 4) % 8
        for oc in (0, 1):
            j = 2 * o + oc
            for cc in (0, 1):
                if wait:
                    arrived(rel.at[a, n, oc, cc], rr.at[a, n, oc, cc])
                act(
                    rcopy(
                        rel.at[a, n, oc, cc], buf.at[rows_of(j)], fs.at[a, n, oc, cc], rs.at[a, j], 2 * w + cc
                    )
                )

            @pl.when(w % 3 != 0)
            def _():
                if wait:
                    arrived(relx.at[a, n, oc], rrx.at[a, n, oc])
                act(rcopy(relx.at[a, n, oc], bx.at[rows_of(j)], fsx.at[a, n, oc], rx.at[a, j], 2 * w))

    def relay(a):
        def pass_on(n, carry):
            forward(a, n, start, True)
            return carry

        lax.fori_loop(0, 3, pass_on, 0)

    @pl.when(i == RELAY)
    def _():
        relay(0)
        relay(1)
        relay(2)

    @pl.when(i == COUNTER)
    def _():
        lane = lax.broadcasted_iota(jnp.int32, (8, 128), 1)
        mine = jnp.zeros((8, 128), jnp.int32)
        for m in range(4):
            mine = jnp.where(lane == 4 * cl + m, counts[m], mine)
        ybuf[y] = mine

        def ycopy(dy):
            return pltpu.make_async_remote_copy(
                ybuf.at[y],
                ybuf.at[y],
                ysend.at[dy],
                yrecv.at[y],
                device_id={"clip": x * ny + (y + dy) % ny},
                device_id_type=MESH,
            )

        def xcopy(dx):
            return pltpu.make_async_remote_copy(
                xbuf.at[x],
                xbuf.at[x],
                xsend.at[dx],
                xrecv.at[x],
                device_id={"clip": ((x + dx) % nx) * ny + y},
                device_id_type=MESH,
            )

        for dy in range(1, ny):
            ycopy(dy).start()
        for dy in range(1, ny):
            o = (y + dy) % ny
            arrived(ybuf.at[o], yrecv.at[o])
        xbuf[x] = jnp.sum(ybuf[...], axis=0)
        for dx in range(1, nx):
            xcopy(dx).start()
        for dx in range(1, nx):
            o = (x + dx) % nx
            arrived(xbuf.at[o], xrecv.at[o])
        pool = jnp.sum(xbuf[...], axis=0)
        picked = jnp.where(lane == assignment[0], pool, 0).astype(F32)
        length = jnp.sum(picked, axis=1, keepdims=True) * float(FRAME_TOK)
        lenb[...] = jnp.broadcast_to(length, (8, WIDE))

        def publish(n, carry):
            rcopy(lenb, lenb, lsend.at[n], lrecv.at[0], n).start()
            return carry

        lax.fori_loop(0, 14, publish, 0)
        for dy in range(1, ny):
            ycopy(dy).wait_send()
        for dx in range(1, nx):
            xcopy(dx).wait_send()

        def published(n, carry):
            rcopy(lenb, lenb, lsend.at[n], lrecv.at[0], n).wait_send()
            return carry

        lax.fori_loop(0, 14, published, 0)

    @pl.when(i < 14)
    def _():
        arrived(lenb, lrecv.at[0])
        for n in range(1, 4):
            part = pl.ds(n * FRAME_TOK, FRAME_TOK)
            live = positions((FRAME_TOK, HD), 0) + float(n * FRAME_TOK) < lenb[0:1, 0:HD]
            for h in range(3):

                def patch(h=h):
                    first = kr[h, 0:16].astype(F32)[0:1]
                    kr[h, part] = jnp.where(live, kr[h, part].astype(F32), first).astype(BF)

                if h < 2:
                    patch()
                else:
                    pl.when(has_x)(patch)

        def v_step(tt, carry):
            w = chip_at((8 - tt) % 8)

            @pl.when(w != 7)
            def _():
                part = pl.ds(pl.multiple_of(w * WIDE, WIDE), WIDE)
                await_block(1, w)
                pos = positions((1, WIDE), 1) + (w * WIDE).astype(F32)
                live = pos < lenb[0:1]
                ones = jnp.broadcast_to(jnp.where(live, 1.0, 0.0), (16, WIDE)).astype(BF)

                def put(h, block):
                    turned = jnp.transpose(block.astype(F32))
                    vt[h, 0:HD, part] = jnp.where(live, turned, 0.0).astype(BF)
                    vt[h, HD : HD + 16, part] = ones

                for h in (0, 1):
                    put(h, vb[part, h * HD : (h + 1) * HD])

                @pl.when(has_x)
                def _():
                    put(2, vx[part])

            return carry

        lax.fori_loop(0, 8, v_step, 0)

        def q_step(tt, carry):
            perm = [0, 2, 3, 1, 4, 5, 6, 7]
            t = perm[7]
            for step in range(7):
                t = jnp.where(tt == step, perm[step], t)
            w = chip_at(t)

            @pl.when(w != 7)
            def _():
                part = pl.ds(pl.multiple_of(w * WIDE, WIDE), WIDE)
                await_block(2, w)
                for h in (0, 1):
                    lanes = slice(h * HD, (h + 1) * HD)
                    ob[part, lanes] = attend(h, qb[part, lanes], w, 2 * i + h)

                @pl.when(has_x)
                def _():
                    ox[part] = attend(2, qx[part], w, 28 + my_e)

                each_result(w, t, start)

            return carry

        lax.fori_loop(0, 8, q_step, 0)

        own = [pltpu.make_async_copy(ob.at[rows_of(i)], out.at[0, :, cols(256 * i, 256)], loc.at[1])]
        own[0].start()
        own_x = pltpu.make_async_copy(
            ox.at[rows_of(i)], out.at[0, :, cols(EXTRA0 + 128 * my_e, 128)], loc.at[2]
        )

        @pl.when(has_x)
        def _():
            own_x.start()

        for a in range(3):
            each_send(a, lambda copy: copy.wait_send())

        def drain(t, carry):
            w = chip_at(t)

            @pl.when(w != 7)
            def _():
                each_result(w, t, lambda copy: copy.wait_send())

            return carry

        lax.fori_loop(0, 8, drain, 0)
        own[0].wait()

        @pl.when(has_x)
        def _():
            own_x.wait()

        def gather(j, carry):
            @pl.when(j != i)
            def _():
                arrived(out.at[0, :, cols(256 * j, 256)], ro.at[j])

            return carry

        lax.fori_loop(0, 14, gather, 0)

        def gather_x(e, carry):
            @pl.when(jnp.logical_not(has_x & (e == my_e)))
            def _():
                arrived(out.at[0, :, cols(EXTRA0 + 128 * e, 128)], rox.at[e])

            return carry

        lax.fori_loop(0, 4, gather_x, 0)

    @pl.when(i >= 14)
    def _():
        zbuf[...] = jnp.zeros_like(zbuf)
        blank = [
            pltpu.make_async_copy(zbuf, out.at[0, n * 16 : (n + 1) * 16], loc.at[n])
            for n in range(8)
        ]
        for copy in blank:
            copy.start()
        for copy in blank:
            copy.wait()

    @pl.when(i == RELAY)
    def _():
        def forward_result(n, act, wait):
            o = source_of(n)
            w = (o + 4) % 8
            e = o - 1 - o // 3
            for cc in (0, 1):
                for oc in (0, 1):
                    j = 2 * o + oc
                    if wait:
                        arrived(relo.at[n, oc, cc], rro.at[n, oc, cc])
                    act(
                        rcopy(
                            relo.at[n, oc, cc],
                            out.at[0, :, cols(256 * j, 256)],
                            fso.at[n, oc, cc],
                            ro.at[j],
                            2 * w + cc,
                        )
                    )

                @pl.when(o % 3 != 0)
                def _():
                    if wait:
                        arrived(relox.at[n, cc], rrox.at[n, cc])
                    act(
                        rcopy(
                            relox.at[n, cc],
                            out.at[0, :, cols(EXTRA0 + 128 * e, 128)],
                            fsox.at[n, cc],
                            rox.at[e],
                            2 * w + cc,
                        )
                    )

        def pass_result(n, carry):
            forward_result(n, start, True)
            return carry

        lax.fori_loop(0, 3, pass_result, 0)

        def finish(n, carry):
            for a in range(3):
                forward(a, n, lambda copy: copy.wait_send(), False)
            forward_result(n, lambda copy: copy.wait_send(), False)
            return carry

        lax.fori_loop(0, 3, finish, 0)


def build(mesh):
    clips = mesh.shape["clip"]
    ny = min(8, clips)
    nx = clips // ny
    dma = pltpu.SemaphoreType.DMA

    def local(queries, keys, values, frame_counts, assignment, timesteps, gate_gain):
        def call(*args):
            kernel(nx, ny, *args)

        anywhere = pl.BlockSpec(memory_space=pl.ANY)
        scalars = pl.BlockSpec(memory_space=pltpu.SMEM)
        return pl.pallas_call(
            call,
            out_shape=pltpu.VMEM(queries.shape, BF),
            in_specs=[anywhere] * 3
            + [scalars] * 3
            + [pl.BlockSpec(memory_space=pltpu.VMEM), anywhere],
            out_specs=pl.BlockSpec(memory_space=pltpu.VMEM),
            scratch_shapes=[pltpu.VMEM((LIVE, 256), BF)] * 4
            + [pltpu.VMEM((LIVE, HD), BF)] * 4
            + [
                pltpu.VMEM((3, LIVE, HD), BF),
                pltpu.VMEM((3, HD + 16, LIVE), BF),
                pltpu.VMEM((3, LIVE, WIDE), F32),
                pltpu.VMEM((3, 3, 2, 2, TOK, 256), BF),
                pltpu.VMEM((3, 3, 2, TOK, HD), BF),
                pltpu.VMEM((3, 2, 2, TOK, 256), BF),
                pltpu.VMEM((3, 2, TOK, HD), BF),
                pltpu.VMEM((ny, 8, 128), jnp.int32),
                pltpu.VMEM((nx, 8, 128), jnp.int32),
                pltpu.VMEM((2, LIVE, HD), F32),
                pltpu.VMEM((8, WIDE), F32),
                pltpu.VMEM((16, 4096), BF),
                dma((3, 14)),
                dma((3, 4)),
                dma((3, 14)),
                dma((3, 14)),
                dma((14,)),
                dma((14,)),
                dma((14,)),
                dma((4,)),
                dma((3, 3, 2, 2)),
                dma((3, 3, 2)),
                dma((3, 3, 2, 2)),
                dma((3, 3, 2)),
                dma((3, 2, 2)),
                dma((3, 2)),
                dma((3, 2, 2)),
                dma((3, 2)),
                dma((8,)),
                dma((8,)),
                dma((4,)),
                dma((4,)),
                dma((8,)),
                dma((14,)),
                dma((1,)),
                pltpu.SemaphoreType.REGULAR((16,)),
            ],
            compiler_params=pltpu.CompilerParams(
                collective_id=0, has_side_effects=True, vmem_limit_bytes=62 * 2**20
            ),
            cost_estimate=pl.CostEstimate(
                flops=4 * 1792 * 1792 * 256,
                bytes_accessed=8 * 2**20,
                transcendentals=2 * 1792 * 1792,
            ),
        )(
            queries,
            keys,
            values,
            frame_counts,
            assignment,
            timesteps,
            gate_gain.reshape(32, HD),
            jnp.asarray(rope_tables()),
        )

    tokens = P("clip", "seq", None)
    return jax.shard_map(
        local,
        mesh=mesh,
        in_specs=(tokens, tokens, tokens, P("clip"), P("clip"), P("clip"), P()),
        out_specs=tokens,
        check_vma=False,
    )


def solution(mesh):
    return build(mesh)
```

```python
import math

import jax
import jax.numpy as jnp
import numpy as np
from jax import lax
from jax.experimental import pallas as pl
from jax.experimental.pallas import tpu as pltpu
from jax.sharding import PartitionSpec as P

HD = 128
FRAME_TOK = 448
GRID_W = 28
LIVE = 1792
TOK = 128
EXTRA0 = 3584
COUNTER = 14
RELAY = 15
MESH = pl.DeviceIdType.MESH
EXP_SCALE = HD ** (-0.5) * math.log2(math.e)
BF = jnp.bfloat16
F32 = jnp.float32
WIDE = 256


def rope_tables():
    position = np.arange(LIVE)
    frame = (position // FRAME_TOK).astype(np.float32)
    within = position % FRAME_TOK
    row_pos = (within // GRID_W).astype(np.float32)
    col_pos = (within % GRID_W).astype(np.float32)
    inv_time = 10000.0 ** (-2.0 * np.arange(22) / 44.0)
    inv_space = 10000.0 ** (-2.0 * np.arange(21) / 42.0)
    angles = np.concatenate(
        [
            frame[:, None] * inv_time[None, :],
            row_pos[:, None] * inv_space[None, :],
            col_pos[:, None] * inv_space[None, :],
        ],
        axis=1,
    )
    cosine, sine = np.cos(angles), np.sin(angles)
    table = np.stack(
        [np.concatenate([cosine, cosine], axis=1), np.concatenate([-sine, sine], axis=1)]
    )
    return table.astype(np.float32)


def kernel(
    nx,
    ny,
    q,
    k,
    v,
    counts,
    assignment,
    timesteps,
    gain,
    table,
    out,
    qb,
    kb,
    vb,
    ob,
    qx,
    kx,
    vx,
    ox,
    kr,
    vt,
    sbuf,
    rel,
    relx,
    relo,
    relox,
    ybuf,
    xbuf,
    tab,
    lenb,
    zbuf,
    ss,
    sx,
    rs,
    rx,
    so,
    sox,
    ro,
    rox,
    rr,
    rrx,
    fs,
    fsx,
    rro,
    rrox,
    fso,
    fsox,
    ysend,
    yrecv,
    xsend,
    xrecv,
    loc,
    lsend,
    lrecv,
    ready,
):
    cl = lax.axis_index("clip")
    i = lax.axis_index("seq")
    z = i // 2
    c = i % 2
    y = cl % ny
    x = cl // ny
    has_x = (c == 0) & (z % 3 != 1) & (z < 6)
    slot = z // 2
    relayed = (z == 0) | (z == 2) | (z == 5)
    my_e = (z - (z + 1) // 3) % 4

    def chip_at(t):
        mag = (4 - t // 2) * ((t + 7) // 8)
        return (z + mag * (1 - 2 * (t % 2)) + 8) % 8

    def rcopy(src, dst, send, recv, j):
        return pltpu.make_async_remote_copy(
            src, dst, send, recv, device_id={"seq": j}, device_id_type=MESH
        )

    def arrived(view, sem):
        pltpu.make_async_copy(view, view, sem).wait()

    def rows_of(j, n=TOK):
        return pl.ds(pl.multiple_of(j * n, n), n)

    def cols(start, n):
        return pl.ds(pl.multiple_of(start, 128), n)

    barrier = pltpu.get_barrier_semaphore()

    def greet(axis, j):
        pl.semaphore_signal(barrier, inc=1, device_id={axis: j}, device_id_type=MESH)

    def tell(j):
        pl.semaphore_signal(ready.at[i], inc=1, device_id={"seq": j}, device_id_type=MESH)

    near = ny - 1 + nx - 1

    @pl.when(i == COUNTER)
    def _():
        for dy in range(1, ny):
            greet("clip", x * ny + (y + dy) % ny)
        for dx in range(1, nx):
            greet("clip", ((x + dx) % nx) * ny + y)

    @pl.when(i < 14)
    def _():
        def one(n, carry):
            @pl.when(n > i)
            def _():
                greet("seq", n)

            return carry

        lax.fori_loop(0, 16, one, 0)

        @pl.when(i > 0)
        def _():
            pl.semaphore_wait(barrier, i)

        def back(n, carry):
            @pl.when(n < i)
            def _():
                tell(n)

            return carry

        lax.fori_loop(0, 14, back, 0)

    @pl.when(i == COUNTER)
    def _():
        pl.semaphore_wait(barrier, 14 + near)

    @pl.when(i == RELAY)
    def _():
        pl.semaphore_wait(barrier, 14)
        for o in (0, 2, 5):
            for cc in (0, 1):
                tell(2 * o + cc)

    arrays = ((k, kb, kx), (v, vb, vx), (q, qb, qx))

    def each_send(a, act, first=False):
        src, buf, bx = arrays[a]

        def one(tt, carry):
            w = chip_at((tt + 1) % 8)
            e = w - (w + 1) // 3
            via = (w == (z + 4) % 8) & relayed

            @pl.when(w != 7)
            def _():
                for cc in (0, 1):
                    j = 2 * w + cc
                    piece = src.at[0, :, cols(256 * j, 256)]
                    if first:

                        @pl.when(j > i)
                        def _():
                            pl.semaphore_wait(ready.at[j], 1)

                        if cc == 0:

                            @pl.when(via)
                            def _():
                                pl.semaphore_wait(ready.at[RELAY], 1)

                    @pl.when(via)
                    def _():
                        act(rcopy(piece, rel.at[a, slot, c, cc], ss.at[a, j], rr.at[a, slot, c, cc], RELAY))

                    @pl.when((j != i) & jnp.logical_not(via))
                    def _():
                        act(rcopy(piece, buf.at[rows_of(i)], ss.at[a, j], rs.at[a, i], j))

                @pl.when((w % 3 != 1) & (w < 6))
                def _():
                    piece = src.at[0, :, cols(EXTRA0 + 128 * e, 128)]

                    @pl.when(via)
                    def _():
                        act(rcopy(piece, relx.at[a, slot, c], sx.at[a, e], rrx.at[a, slot, c], RELAY))

                    @pl.when((2 * w != i) & jnp.logical_not(via))
                    def _():
                        act(rcopy(piece, bx.at[rows_of(i)], sx.at[a, e], rx.at[a, i], 2 * w))

            return carry

        lax.fori_loop(0, 8, one, 0)

    def own_copy(a):
        src, buf, bx = arrays[a]
        pltpu.make_async_copy(
            src.at[0, :, cols(256 * i, 256)], buf.at[rows_of(i)], rs.at[a, i]
        ).start()

        @pl.when(has_x)
        def _():
            pltpu.make_async_copy(
                src.at[0, :, cols(EXTRA0 + 128 * my_e, 128)], bx.at[rows_of(i)], rx.at[a, i]
            ).start()

    def await_block(a, w):
        _, buf, bx = arrays[a]
        for cc in (0, 1):
            j = 2 * w + cc
            arrived(buf.at[rows_of(j)], rs.at[a, j])

            @pl.when(has_x)
            def _():
                arrived(bx.at[rows_of(j)], rx.at[a, j])

    def turn(block, w):
        part = pl.ds(pl.multiple_of(w * WIDE, WIDE), WIDE)
        return block * tab[0, part] + pltpu.roll(block, HD // 2, 1) * tab[1, part]

    def positions(shape, dim):
        return lax.broadcasted_iota(jnp.int32, shape, dim).astype(F32)

    def start(copy):
        copy.start()

    def each_result(w, t, act):
        via = (t == 1) & relayed
        for cc in (0, 1):
            j = 2 * w + cc
            rows = rows_of(j)

            @pl.when(via)
            def _():
                act(rcopy(ob.at[rows], relo.at[slot, c, cc], so.at[j], rro.at[slot, c, cc], RELAY))

                @pl.when(has_x)
                def _():
                    act(rcopy(ox.at[rows], relox.at[slot, cc], sox.at[j], rrox.at[slot, cc], RELAY))

            @pl.when((j != i) & jnp.logical_not(via))
            def _():
                act(rcopy(ob.at[rows], out.at[0, :, cols(256 * i, 256)], so.at[j], ro.at[i], j))

                @pl.when(has_x)
                def _():
                    act(
                        rcopy(
                            ox.at[rows],
                            out.at[0, :, cols(EXTRA0 + 128 * my_e, 128)],
                            sox.at[j],
                            rox.at[my_e],
                            j,
                        )
                    )

    def gate_of(head):
        fraction = jnp.full((1, HD), timesteps[0], jnp.int32).astype(F32) / 1000.0
        sigma = 5.0 * fraction / (1.0 + 4.0 * fraction)
        return 1.0 + sigma * gain[pl.ds(head, 1), :]

    def attend(h, block, w, head):
        q_rot = turn(block.astype(F32), w).astype(BF)
        top = None
        for n in range(LIVE // WIDE):
            part = pl.ds(n * WIDE, WIDE)
            s = lax.dot_general(
                kr[h, part], q_rot, (((1,), (1,)), ((), ())), preferred_element_type=F32
            )
            sbuf[h, part] = s
            high = jnp.max(s.reshape(WIDE // 8, 8, WIDE), axis=0)
            top = high if top is None else jnp.maximum(top, high)
        top = jnp.max(top, axis=0, keepdims=True)
        total = None
        for n in range(LIVE // WIDE):
            part = pl.ds(n * WIDE, WIDE)
            p = jnp.exp2((sbuf[h, part] - top) * EXP_SCALE).astype(BF)
            term = jnp.dot(vt[h, :, part], p, preferred_element_type=F32)
            total = term if total is None else total + term
        mixed = total[:HD] * (1.0 / total[HD : HD + 1])
        mixed = jnp.transpose(mixed).astype(BF).astype(F32)
        pos = positions((WIDE, HD), 0) + (w * WIDE).astype(F32)
        return jnp.where(pos < lenb[0:1, 0:HD], mixed * gate_of(head), 0.0).astype(BF)

    @pl.when(i < 14)
    def _():
        table_copy = pltpu.make_async_copy(table, tab, loc.at[0])
        table_copy.start()
        for a in range(3):
            each_send(a, start, a == 0)
            own_copy(a)
        table_copy.wait()

        def k_step(tt, carry):
            w = chip_at((8 - tt) % 8)

            @pl.when(w != 7)
            def _():
                part = pl.ds(pl.multiple_of(w * WIDE, WIDE), WIDE)
                await_block(0, w)
                for h in (0, 1):
                    kr[h, part] = turn(kb[part, h * HD : (h + 1) * HD].astype(F32), w).astype(BF)

                @pl.when(has_x)
                def _():
                    kr[2, part] = turn(kx[part].astype(F32), w).astype(BF)

            return carry

        lax.fori_loop(0, 8, k_step, 0)

    def source_of(n):
        return 2 * n + n // 2

    def forward(a, n, act, wait):
        _, buf, bx = arrays[a]
        o = source_of(n)
        w = (o + 4) % 8
        for oc in (0, 1):
            j = 2 * o + oc
            for cc in (0, 1):
                if wait:
                    arrived(rel.at[a, n, oc, cc], rr.at[a, n, oc, cc])
                act(
                    rcopy(
                        rel.at[a, n, oc, cc], buf.at[rows_of(j)], fs.at[a, n, oc, cc], rs.at[a, j], 2 * w + cc
                    )
                )

            @pl.when((w % 3 != 1) & (w < 6))
            def _():
                if wait:
                    arrived(relx.at[a, n, oc], rrx.at[a, n, oc])
                act(rcopy(relx.at[a, n, oc], bx.at[rows_of(j)], fsx.at[a, n, oc], rx.at[a, j], 2 * w))

    def relay(a):
        def pass_on(n, carry):
            forward(a, n, start, True)
            return carry

        lax.fori_loop(0, 3, pass_on, 0)

    @pl.when(i == RELAY)
    def _():
        relay(0)
        relay(1)
        relay(2)

    @pl.when(i == COUNTER)
    def _():
        lane = lax.broadcasted_iota(jnp.int32, (8, 128), 1)
        mine = jnp.zeros((8, 128), jnp.int32)
        for m in range(4):
            mine = jnp.where(lane == 4 * cl + m, counts[m], mine)
        ybuf[y] = mine

        def ycopy(dy):
            return pltpu.make_async_remote_copy(
                ybuf.at[y],
                ybuf.at[y],
                ysend.at[dy],
                yrecv.at[y],
                device_id={"clip": x * ny + (y + dy) % ny},
                device_id_type=MESH,
            )

        def xcopy(dx):
            return pltpu.make_async_remote_copy(
                xbuf.at[x],
                xbuf.at[x],
                xsend.at[dx],
                xrecv.at[x],
                device_id={"clip": ((x + dx) % nx) * ny + y},
                device_id_type=MESH,
            )

        for dy in range(1, ny):
            ycopy(dy).start()
        for dy in range(1, ny):
            o = (y + dy) % ny
            arrived(ybuf.at[o], yrecv.at[o])
        xbuf[x] = jnp.sum(ybuf[...], axis=0)
        for dx in range(1, nx):
            xcopy(dx).start()
        for dx in range(1, nx):
            o = (x + dx) % nx
            arrived(xbuf.at[o], xrecv.at[o])
        pool = jnp.sum(xbuf[...], axis=0)
        picked = jnp.where(lane == assignment[0], pool, 0).astype(F32)
        length = jnp.sum(picked, axis=1, keepdims=True) * float(FRAME_TOK)
        lenb[...] = jnp.broadcast_to(length, (8, WIDE))

        def publish(n, carry):
            rcopy(lenb, lenb, lsend.at[n], lrecv.at[0], n).start()
            return carry

        lax.fori_loop(0, 14, publish, 0)
        for dy in range(1, ny):
            ycopy(dy).wait_send()
        for dx in range(1, nx):
            xcopy(dx).wait_send()

        def published(n, carry):
            rcopy(lenb, lenb, lsend.at[n], lrecv.at[0], n).wait_send()
            return carry

        lax.fori_loop(0, 14, published, 0)

    @pl.when(i < 14)
    def _():
        arrived(lenb, lrecv.at[0])
        for n in range(1, 4):
            part = pl.ds(n * FRAME_TOK, FRAME_TOK)
            live = positions((FRAME_TOK, HD), 0) + float(n * FRAME_TOK) < lenb[0:1, 0:HD]
            for h in range(3):

                def patch(h=h):
                    first = kr[h, 0:16].astype(F32)[0:1]
                    kr[h, part] = jnp.where(live, kr[h, part].astype(F32), first).astype(BF)

                if h < 2:
                    patch()
                else:
                    pl.when(has_x)(patch)

        def v_step(tt, carry):
            w = chip_at((8 - tt) % 8)

            @pl.when(w != 7)
            def _():
                part = pl.ds(pl.multiple_of(w * WIDE, WIDE), WIDE)
                await_block(1, w)
                pos = positions((1, WIDE), 1) + (w * WIDE).astype(F32)
                live = pos < lenb[0:1]
                ones = jnp.broadcast_to(jnp.where(live, 1.0, 0.0), (16, WIDE)).astype(BF)

                def put(h, block):
                    turned = jnp.transpose(block.astype(F32))
                    vt[h, 0:HD, part] = jnp.where(live, turned, 0.0).astype(BF)
                    vt[h, HD : HD + 16, part] = ones

                for h in (0, 1):
                    put(h, vb[part, h * HD : (h + 1) * HD])

                @pl.when(has_x)
                def _():
                    put(2, vx[part])

            return carry

        lax.fori_loop(0, 8, v_step, 0)

        def q_step(tt, carry):
            perm = [0, 2, 3, 1, 4, 5, 6, 7]
            t = perm[7]
            for step in range(7):
                t = jnp.where(tt == step, perm[step], t)
            w = chip_at(t)

            @pl.when(w != 7)
            def _():
                part = pl.ds(pl.multiple_of(w * WIDE, WIDE), WIDE)
                await_block(2, w)
                for h in (0, 1):
                    lanes = slice(h * HD, (h + 1) * HD)
                    ob[part, lanes] = attend(h, qb[part, lanes], w, 2 * i + h)

                @pl.when(has_x)
                def _():
                    ox[part] = attend(2, qx[part], w, 28 + my_e)

                each_result(w, t, start)

            return carry

        lax.fori_loop(0, 8, q_step, 0)

        own = [pltpu.make_async_copy(ob.at[rows_of(i)], out.at[0, :, cols(256 * i, 256)], loc.at[1])]
        own[0].start()
        own_x = pltpu.make_async_copy(
            ox.at[rows_of(i)], out.at[0, :, cols(EXTRA0 + 128 * my_e, 128)], loc.at[2]
        )

        @pl.when(has_x)
        def _():
            own_x.start()

        for a in range(3):
            each_send(a, lambda copy: copy.wait_send())

        def drain(t, carry):
            w = chip_at(t)

            @pl.when(w != 7)
            def _():
                each_result(w, t, lambda copy: copy.wait_send())

            return carry

        lax.fori_loop(0, 8, drain, 0)
        own[0].wait()

        @pl.when(has_x)
        def _():
            own_x.wait()

        def gather(j, carry):
            @pl.when(j != i)
            def _():
                arrived(out.at[0, :, cols(256 * j, 256)], ro.at[j])

            return carry

        lax.fori_loop(0, 14, gather, 0)

        def gather_x(e, carry):
            @pl.when(jnp.logical_not(has_x & (e == my_e)))
            def _():
                arrived(out.at[0, :, cols(EXTRA0 + 128 * e, 128)], rox.at[e])

            return carry

        lax.fori_loop(0, 4, gather_x, 0)

    @pl.when(i >= 14)
    def _():
        zbuf[...] = jnp.zeros_like(zbuf)
        blank = [
            pltpu.make_async_copy(zbuf, out.at[0, n * 16 : (n + 1) * 16], loc.at[n])
            for n in range(8)
        ]
        for copy in blank:
            copy.start()
        for copy in blank:
            copy.wait()

    @pl.when(i == RELAY)
    def _():
        def forward_result(n, act, wait):
            o = source_of(n)
            w = (o + 4) % 8
            e = o - (o + 1) // 3
            for cc in (0, 1):
                for oc in (0, 1):
                    j = 2 * o + oc
                    if wait:
                        arrived(relo.at[n, oc, cc], rro.at[n, oc, cc])
                    act(
                        rcopy(
                            relo.at[n, oc, cc],
                            out.at[0, :, cols(256 * j, 256)],
                            fso.at[n, oc, cc],
                            ro.at[j],
                            2 * w + cc,
                        )
                    )

                @pl.when((o % 3 != 1) & (o < 6))
                def _():
                    if wait:
                        arrived(relox.at[n, cc], rrox.at[n, cc])
                    act(
                        rcopy(
                            relox.at[n, cc],
                            out.at[0, :, cols(EXTRA0 + 128 * e, 128)],
                            fsox.at[n, cc],
                            rox.at[e],
                            2 * w + cc,
                        )
                    )

        def pass_result(n, carry):
            forward_result(n, start, True)
            return carry

        lax.fori_loop(0, 3, pass_result, 0)

        def finish(n, carry):
            for a in range(3):
                forward(a, n, lambda copy: copy.wait_send(), False)
            forward_result(n, lambda copy: copy.wait_send(), False)
            return carry

        lax.fori_loop(0, 3, finish, 0)


def build(mesh):
    clips = mesh.shape["clip"]
    ny = min(8, clips)
    nx = clips // ny
    dma = pltpu.SemaphoreType.DMA

    def local(queries, keys, values, frame_counts, assignment, timesteps, gate_gain):
        def call(*args):
            kernel(nx, ny, *args)

        anywhere = pl.BlockSpec(memory_space=pl.ANY)
        scalars = pl.BlockSpec(memory_space=pltpu.SMEM)
        return pl.pallas_call(
            call,
            out_shape=pltpu.VMEM(queries.shape, BF),
            in_specs=[anywhere] * 3
            + [scalars] * 3
            + [pl.BlockSpec(memory_space=pltpu.VMEM), anywhere],
            out_specs=pl.BlockSpec(memory_space=pltpu.VMEM),
            scratch_shapes=[pltpu.VMEM((LIVE, 256), BF)] * 4
            + [pltpu.VMEM((LIVE, HD), BF)] * 4
            + [
                pltpu.VMEM((3, LIVE, HD), BF),
                pltpu.VMEM((3, HD + 16, LIVE), BF),
                pltpu.VMEM((3, LIVE, WIDE), F32),
                pltpu.VMEM((3, 3, 2, 2, TOK, 256), BF),
                pltpu.VMEM((3, 3, 2, TOK, HD), BF),
                pltpu.VMEM((3, 2, 2, TOK, 256), BF),
                pltpu.VMEM((3, 2, TOK, HD), BF),
                pltpu.VMEM((ny, 8, 128), jnp.int32),
                pltpu.VMEM((nx, 8, 128), jnp.int32),
                pltpu.VMEM((2, LIVE, HD), F32),
                pltpu.VMEM((8, WIDE), F32),
                pltpu.VMEM((16, 4096), BF),
                dma((3, 14)),
                dma((3, 4)),
                dma((3, 14)),
                dma((3, 14)),
                dma((14,)),
                dma((14,)),
                dma((14,)),
                dma((4,)),
                dma((3, 3, 2, 2)),
                dma((3, 3, 2)),
                dma((3, 3, 2, 2)),
                dma((3, 3, 2)),
                dma((3, 2, 2)),
                dma((3, 2)),
                dma((3, 2, 2)),
                dma((3, 2)),
                dma((8,)),
                dma((8,)),
                dma((4,)),
                dma((4,)),
                dma((8,)),
                dma((14,)),
                dma((1,)),
                pltpu.SemaphoreType.REGULAR((16,)),
            ],
            compiler_params=pltpu.CompilerParams(
                collective_id=0, has_side_effects=True, vmem_limit_bytes=62 * 2**20
            ),
            cost_estimate=pl.CostEstimate(
                flops=4 * 1792 * 1792 * 256,
                bytes_accessed=8 * 2**20,
                transcendentals=2 * 1792 * 1792,
            ),
        )(
            queries,
            keys,
            values,
            frame_counts,
            assignment,
            timesteps,
            gate_gain.reshape(32, HD),
            jnp.asarray(rope_tables()),
        )

    tokens = P("clip", "seq", None)
    return jax.shard_map(
        local,
        mesh=mesh,
        in_specs=(tokens, tokens, tokens, P("clip"), P("clip"), P("clip"), P()),
        out_specs=tokens,
        check_vma=False,
    )


def solution(mesh):
    return build(mesh)
```
